128 devices in a mesh: seq: 8 (over z, core), ch: 16 (over y, x).
Axes of the slice: x: 4, y: 4, z: 4, core: 2. Of those that a mesh axis runs over, the one named last changes fastest.
Arguments:
- key_branch: bfloat16 [4096, 4096], P('seq', 'ch'), may hold values from -6 to 6
- value_branch: bfloat16 [4096, 4096], P('seq', 'ch'), may hold values from -6 to 6
- gate_branch: bfloat16 [4096, 4096], P('seq', 'ch'), may hold values from -6 to 6
- conv_filter: bfloat16 [4096, 4096], P('seq', 'ch'), may hold values from -0.5 to 0.5, as said below
- skip_gain: float32 [4096], P('ch'), may hold values from -4 to 4
Outputs:
- output: bfloat16 [4096, 4096], P('seq', 'ch')
The draws below stay inside these ranges and needn't reach their ends.
Inputs may be any that keep to these rules, and one draw needn't show every extreme that they name: `conv_filter`: one filter value per position and channel.
All inputs are finite; a program needn't handle non-finite values.
Results may differ from the reference program's by a relative error of at most 0.0049.
Values may be sent and summed in bfloat16 or wider, within the bound.
No kernel may reach another device: no remote copies, remote signals or barrier semaphores. Data moves between devices by JAX's collectives and lax.ppermute only.
A program may use at most 128 MiB of HBM per device.

```python
import math
import jax
import jax.numpy as jnp
from jax import lax

C = 4096
LEN = 4096


def draw_conv_filter(key, part):
    key = jax.random.fold_in(key, 11)
    subkeys = jax.random.split(key, 4)
    positions = jnp.arange(LEN, dtype=jnp.float32)[:, None]
    quick_rate = jnp.exp(jax.random.uniform(subkeys[0], (C,), jnp.float32, math.log(1.0 / 40.0), math.log(1.0 / 8.0)))
    lowest, highest = (0.1, 40.0)
    slow_rate = jnp.exp(jax.random.uniform(subkeys[1], (C,), jnp.float32, math.log(lowest / LEN), math.log(highest / LEN)))
    sign_values = jax.random.rademacher(subkeys[2], (2, C), dtype=jnp.float32)
    quick_amp = 0.6 * jnp.sqrt(2.0 * quick_rate) * sign_values[0]
    slow_amp = jnp.sqrt(2.0 * slow_rate + 1.0 / LEN) * sign_values[1]
    roughness = 1.0 + 0.5 * jax.random.uniform(subkeys[3], (LEN, C), jnp.float32, -1.0, 1.0)
    envelope = quick_amp[None, :] * jnp.exp(-quick_rate[None, :] * positions) + slow_amp[None, :] * jnp.exp(-slow_rate[None, :] * positions)
    return jnp.clip(envelope * roughness, -0.5, 0.5).astype(jnp.bfloat16)


def steps_of(own_key, shape, cuts, smallest, high):
    factor_of = 1.0
    for position, blocks in cuts:
        draws = jax.random.uniform(jax.random.fold_in(jax.random.fold_in(own_key, 6), position), (blocks,), jnp.float32, smallest / len(cuts), high / len(cuts))
        factor_of = factor_of * jnp.repeat(jnp.exp(draws), shape[position] // blocks).reshape((-1,) + (1,) * (len(shape) - 1 - position))
    return factor_of


def bell_draw(own_key, shape, deviation, most, pieces=(), kind=jnp.bfloat16):
    values = deviation * jax.random.normal(own_key, shape, jnp.float32)
    if pieces:
        values = values * steps_of(own_key, shape, pieces, -0.22, 0.18)
    return jnp.clip(values, -most, most).astype(kind)


def setup_inputs(seed: int = 0) -> dict:
    streams_of = jax.random.split(jax.random.key(seed), 6)
    key_branch = bell_draw(streams_of[0], (LEN, C), 1.0, 6.0, ((0, 8), (1, 16)))
    value_branch = bell_draw(streams_of[1], (LEN, C), 1.0, 6.0, ((0, 8), (1, 16)))
    gate_branch = bell_draw(streams_of[2], (LEN, C), 1.0, 6.0, ((0, 8), (1, 16)))
    conv_filter = draw_conv_filter(jax.random.fold_in(streams_of[5], 71), 0)
    skip_gain = bell_draw(streams_of[4], (C,), 1.0, 4.0, ((0, 16),), jnp.float32)
    return dict(key_branch=key_branch, value_branch=value_branch, gate_branch=gate_branch, conv_filter=conv_filter, skip_gain=skip_gain)


def reference(key_branch, value_branch, gate_branch, conv_filter, skip_gain):
    product = (key_branch.astype(jnp.float32) * value_branch.astype(jnp.float32)).astype(jnp.bfloat16)
    source = product.astype(jnp.float32)
    kernel = conv_filter.astype(jnp.float32)
    seq_length = source.shape[0]
    channels = source.shape[1]
    group_size = math.gcd(channels, 128)
    group_count = channels // group_size

    def one_group(inputs_pair):
        signal, tap_values = inputs_pair
        spectrum = jnp.fft.rfft(signal, n=2 * seq_length, axis=0) * jnp.fft.rfft(tap_values, n=2 * seq_length, axis=0)
        return jnp.fft.irfft(spectrum, n=2 * seq_length, axis=0)[:seq_length].astype(source.dtype)

    grouped_source = source.reshape(seq_length, group_count, group_size).transpose(1, 0, 2)
    grouped_taps = kernel.reshape(seq_length, group_count, group_size).transpose(1, 0, 2)
    mixed_conv = lax.map(one_group, (grouped_source, grouped_taps))
    mixed_conv = mixed_conv.transpose(1, 0, 2).reshape(seq_length, channels)
    output = gate_branch.astype(jnp.float32) * (mixed_conv + skip_gain[None, :] * source)
    return output.astype(jnp.bfloat16)
```

```python
import jax
import jax.numpy as jnp
from jax import lax
from jax.experimental import pallas as pl
from jax.experimental.pallas import tpu as pltpu
from jax.sharding import PartitionSpec as P

F32 = jnp.float32
BF16 = jnp.bfloat16
PARTS = 8
CH = 32
VMEM = 48 * 1024 * 1024


def product_of(k, v):
    return (k.astype(F32) * v.astype(F32)).astype(BF16)


def pack_kernel(k_ref, v_ref, f_ref, o_ref):
    p = product_of(k_ref[...], v_ref[...]).astype(F32)
    p = p.reshape(2, 16, 16, 256).transpose(1, 0, 2, 3).reshape(512, 256)
    f = f_ref[...].astype(F32)
    for half in range(2):
        for q in range(4):
            for at, x in ((0, p), (4, f)):
                block = x[128 * q : 128 * q + 128, 128 * half : 128 * half + 128]
                block = block.T.astype(BF16).reshape(4, CH, 128)
                o_ref[4 * half : 4 * half + 4, at + q] = block


def conv_kernel(r_ref, y_ref, g_s, v_s, vv_s, gl_s, a_s, b_s, o_s, y_s):
    lane = lax.broadcasted_iota(jnp.int32, (16, 128), 1)
    row16 = lax.broadcasted_iota(jnp.int32, (16, 128), 0)
    g_s[0:CH] = jnp.zeros((CH, 128), F32)
    for s in range(PARTS):
        for q in range(4):
            g = 4 * s + q + 1
            g_s[CH * g : CH * g + CH] = r_ref[s, 4 + q].astype(F32)
    lane32 = lax.broadcasted_iota(jnp.int32, (CH, 128), 1)
    for x0h in range(4):
        pieces = [r_ref[s, x0h].astype(F32) for s in range(PARTS)]
        for x0l in range(4):
            x0 = 4 * x0h + x0l
            for tile in range(2):
                out = None
                for i in range(4):
                    piece = pieces[4 * tile + i]
                    shift = (32 * i - 32 * x0l) % 128
                    if shift:
                        piece = pltpu.roll(piece, shift, 1)
                    out = piece if out is None else jnp.where(lane32 >= 32 * i, piece, out)
                v_s[tile, CH * x0 : CH * x0 + CH] = out

    def gather(c, carry):
        for tile in range(2):
            vv_s[pl.ds(pl.multiple_of(16 * c, 16), 16), 128 * tile : 128 * tile + 128] = v_s[
                tile, pl.ds(c, 16, stride=CH), :
            ].astype(BF16)
        rows = [g_s[pl.ds(CH * j + c, 16, stride=2 * CH), :].astype(BF16) for j in range(3)]
        for half in range(2):
            at = pl.multiple_of(32 * c + 16 * half, 16)
            gl_s[pl.ds(at, 16), 0:128] = rows[half]
            gl_s[pl.ds(at, 16), 128:256] = rows[half + 1]
        return carry

    lax.fori_loop(0, CH, gather, 0)

    wide_row = lax.broadcasted_iota(jnp.int32, (256, 256), 0)
    wide_col = lax.broadcasted_iota(jnp.int32, (256, 256), 1)

    def expand_a(x1, carry):
        hit = (wide_row % 16 == wide_col // 16) & (wide_row // 16 + wide_col % 16 == x1)
        table = jnp.where(hit, 1.0, 0.0).astype(BF16)
        out = jnp.dot(vv_s[...], table, preferred_element_type=F32).astype(BF16)
        a_s[:, pl.ds(pl.multiple_of(16 * x1, 16), 16), :] = out.reshape(CH, 16, 256)
        return carry

    lax.fori_loop(0, 16, expand_a, 0)

    def expand_b(i, carry):
        hit = wide_row == 128 + wide_col % 128 - (2 * i + wide_col // 128)
        table = jnp.where(hit, 1.0, 0.0).astype(BF16)
        out = jnp.dot(gl_s[...], table, preferred_element_type=F32).astype(BF16)
        out = out.reshape(CH, 2, 16, 256)
        for j in range(2):
            at = pl.multiple_of(32 * i + 16 * j, 16)
            for half in range(2):
                b_s[:, pl.ds(at, 16), 128 * half : 128 * half + 128] = out[
                    :, half, :, 128 * j : 128 * j + 128
                ]
        return carry

    lax.fori_loop(0, 8, expand_b, 0)

    def convolve(c, carry):
        out = jnp.dot(a_s[c], b_s[c], preferred_element_type=F32)
        o_s[0] = out[:, :128]
        o_s[1] = out[:, 128:]
        acc = [jnp.zeros((16, 128), F32) for _ in range(4)]
        for x0 in range(16):
            r0 = o_s[0, pl.ds(x0, 16, stride=16), :]
            r1 = o_s[1, pl.ds(x0, 16, stride=16), :]
            shift, t = 16 * (x0 % 8), x0 // 8
            if shift:
                r0 = pltpu.roll(r0, shift, 1)
                r1 = pltpu.roll(r1, shift, 1)
                low = lane < shift
                acc[t] = acc[t] + jnp.where(low, 0.0, r0)
                acc[t + 1] = acc[t + 1] + jnp.where(low, r0, r1)
                acc[t + 2] = acc[t + 2] + jnp.where(low, r1, 0.0)
            else:
                acc[t] = acc[t] + r0
                acc[t + 1] = acc[t + 1] + r1
        for half in range(2):
            late = jnp.where(row16 == 0, 0.0, pltpu.roll(acc[2 + half], 1, 0))
            y_s[pl.ds(CH * half + c, 16, stride=2 * CH), :] = acc[half] + late
        return carry

    lax.fori_loop(0, CH, convolve, 0)
    for s in range(PARTS):
        for q in range(4):
            g = 4 * s + q
            y_ref[s, q] = y_s[CH * g : CH * g + CH].astype(BF16)


def gate_kernel(y_ref, k_ref, v_ref, g_ref, s_ref, o_ref):
    for half in range(2):
        ch = slice(128 * half, 128 * half + 128)
        for q in range(4):
            pos = slice(128 * q, 128 * q + 128)
            y = y_ref[4 * half : 4 * half + 4, q].reshape(128, 128).astype(F32).T
            p = product_of(k_ref[pos, ch], v_ref[pos, ch]).astype(F32)
            out = g_ref[pos, ch].astype(F32) * (y + s_ref[:, ch] * p)
            o_ref[pos, ch] = out.astype(BF16)


def call(kernel, shape, scratch=(), flops=0):
    return pl.pallas_call(
        kernel,
        out_shape=jax.ShapeDtypeStruct(shape, BF16),
        scratch_shapes=scratch,
        compiler_params=pltpu.CompilerParams(vmem_limit_bytes=VMEM),
    )


def exchange(x):
    return lax.all_to_all(x, "seq", split_axis=0, concat_axis=0, tiled=True)


def on_device(key_branch, value_branch, gate_branch, conv_filter, skip_gain):
    sent = call(pack_kernel, (PARTS, 8, CH, 128))(key_branch, value_branch, conv_filter)
    got = exchange(sent)
    mixed = call(
        conv_kernel,
        (PARTS, 4, CH, 128),
        [
            pltpu.VMEM((33 * CH, 128), F32),
            pltpu.VMEM((2, 16 * CH, 128), F32),
            pltpu.VMEM((16 * CH, 256), BF16),
            pltpu.VMEM((32 * CH, 256), BF16),
            pltpu.VMEM((CH, 256, 256), BF16),
            pltpu.VMEM((CH, 256, 256), BF16),
            pltpu.VMEM((2, 256, 128), F32),
            pltpu.VMEM((32 * CH, 128), F32),
        ],
    )(got)
    back = exchange(mixed)
    return call(gate_kernel, (512, 256))(
        back, key_branch, value_branch, gate_branch, skip_gain.reshape(1, 256)
    )


def solution(mesh):
    in_specs = (P("seq", "ch"), P("seq", "ch"), P("seq", "ch"), P("seq", "ch"), P("ch"))
    return jax.shard_map(
        on_device, mesh=mesh, in_specs=in_specs, out_specs=P("seq", "ch"), check_vma=False
    )
```

```python
import jax
import jax.numpy as jnp
from jax import lax
from jax.experimental import pallas as pl
from jax.experimental.pallas import tpu as pltpu
from jax.sharding import PartitionSpec as P

F32 = jnp.float32
BF16 = jnp.bfloat16
PARTS = 8
CH = 32
AT_ONCE = 4
VMEM = 48 * 1024 * 1024


def product_of(k, v):
    return (k.astype(F32) * v.astype(F32)).astype(BF16)


def pack_kernel(p_ref, f_ref, o_ref):
    p = p_ref[...].astype(F32)
    p = p.reshape(4, 8, 16, 256)
    p = jnp.stack([p[3 - a] for a in range(4)], 1).reshape(512, 256)
    f = f_ref[...].astype(F32)
    for half in range(2):
        for q in range(4):
            for at, x in ((0, p), (4, f)):
                block = x[128 * q : 128 * q + 128, 128 * half : 128 * half + 128]
                block = block.T.astype(BF16).reshape(4, CH, 128)
                o_ref[4 * half : 4 * half + 4, at + q] = block


def conv_kernel(r_ref, s_ref, y_ref, so_ref, g_s, v_s, a_s, b_s, o_s, y_s):
    so_ref[...] = s_ref[...]
    lane = lax.broadcasted_iota(jnp.int32, (32, 128), 1)
    row = lax.broadcasted_iota(jnp.int32, (32, 128), 0)
    for s in range(PARTS):
        for q in range(4):
            g = 4 * s + q
            g_s[CH * g : CH * g + CH] = r_ref[s, 4 + q].astype(F32)
    for q in range(4):
        for j in range(4):
            first, second = [r_ref[s, q].astype(F32) for s in (2 * j + 1, 2 * j)]
            at = 2 * CH * q
            v_s[j, at : at + CH] = jnp.where(lane < 64, first, pltpu.roll(second, 64, 1))
            v_s[j, at + CH : at + 2 * CH] = jnp.where(lane < 64, pltpu.roll(first, 64, 1), second)
    stay_a = lane[:8] < 16 + 16 * row[:8]
    stay_b = lane[:16] >= row[:16]
    zero = jnp.zeros((8, 128), F32)

    def pair(a, b):
        return jnp.concatenate([a, b], 0).astype(BF16)

    def build(c, u):
        prev = jnp.zeros((16, 128), F32)
        for g in range(32):
            taps = jnp.broadcast_to(g_s[pl.ds(CH * g + c, 1), :], (16, 128))
            rot = pltpu.roll(taps, 0, 1, stride=1, stride_axis=0)
            at, half = 16 * (g % 16), 128 * (g // 16)
            b_s[u, at : at + 16, half : half + 128] = jnp.where(stay_b, rot, prev).astype(BF16)
            prev = rot
        for b in range(8):
            prev, w = zero, []
            for j in range(4):
                vals = jnp.broadcast_to(v_s[j, pl.ds(CH * b + c, 1), :], (8, 128))
                rot = pltpu.roll(vals, 16, 1, stride=16, stride_axis=0)
                w.append(jnp.where(stay_a, rot, prev))
                prev = rot
            lo, hi = slice(16 * b, 16 * b + 16), slice(128 + 16 * b, 144 + 16 * b)
            a_s[u, lo, :128] = pair(w[0], w[1])
            a_s[u, lo, 128:] = pair(zero, w[0])
            a_s[u, hi, :128] = pair(w[2], w[3])
            a_s[u, hi, 128:] = pair(w[1], w[2])

    def multiply(u):
        o_s[u] = jnp.dot(a_s[u], b_s[u], preferred_element_type=F32)

    def collect(c, u):
        here = jnp.zeros((32, 128), F32)
        late = jnp.zeros((32, 128), F32)
        for b in range(8):
            lo, hi = slice(16 * b, 16 * b + 16), slice(128 + 16 * b, 144 + 16 * b)
            r = jnp.concatenate([o_s[u, lo, :128], o_s[u, hi, :128] + o_s[u, lo, 128:]], 0)
            if b:
                r = pltpu.roll(r, 16 * b, 1)
                over = lane < 16 * b
                late = late + jnp.where(over, r, 0.0)
                r = jnp.where(over, 0.0, r)
            here = here + r
        late = jnp.where(row == 0, 0.0, pltpu.roll(late, 1, 0))
        y_s[pl.ds(c, 32, stride=CH), :] = here + late

    for u in range(AT_ONCE):
        build(u, u)
    for u in range(AT_ONCE):
        multiply(u)
    for u in range(AT_ONCE):
        build(AT_ONCE + u, u)

    def step(i, carry):
        for u in range(AT_ONCE):
            collect((i - 1) * AT_ONCE + u, u)
            multiply(u)
            build(jnp.minimum((i + 1) * AT_ONCE, CH - AT_ONCE) + u, u)
        return carry

    lax.fori_loop(1, CH // AT_ONCE, step, 0)
    for u in range(AT_ONCE):
        collect(CH - AT_ONCE + u, u)
    for s in range(PARTS):
        for q in range(4):
            g = 4 * s + q
            y_ref[s, q] = y_s[CH * g : CH * g + CH].astype(BF16)


def gate_kernel(y_ref, k_ref, v_ref, g_ref, s_ref, o_ref):
    for half in range(2):
        ch = slice(128 * half, 128 * half + 128)
        for q in range(4):
            pos = slice(128 * q, 128 * q + 128)
            y = y_ref[4 * half : 4 * half + 4, q].reshape(128, 128).astype(F32).T
            p = product_of(k_ref[pos, ch], v_ref[pos, ch]).astype(F32)
            out = g_ref[pos, ch].astype(F32) * (y + s_ref[:, ch] * p)
            o_ref[pos, ch] = out.astype(BF16)


def call(kernel, out, scratch=(), limit=VMEM, **more):
    return pl.pallas_call(
        kernel,
        out_shape=out,
        scratch_shapes=scratch,
        compiler_params=pltpu.CompilerParams(vmem_limit_bytes=limit),
        **more,
    )


def exchange(x):
    return lax.all_to_all(x, "seq", split_axis=0, concat_axis=0, tiled=True)


def on_device(key_branch, value_branch, gate_branch, conv_filter, skip_gain):
    skip_gain = skip_gain.reshape(1, 256)
    sent = call(pack_kernel, jax.ShapeDtypeStruct((PARTS, 8, CH, 128), BF16))(
        product_of(key_branch, value_branch), conv_filter
    )
    got = exchange(sent)
    mixed, skip_gain = call(
        conv_kernel,
        [jax.ShapeDtypeStruct((PARTS, 4, CH, 128), BF16), jax.ShapeDtypeStruct((1, 256), F32)],
        [
            pltpu.VMEM((32 * CH, 128), F32),
            pltpu.VMEM((4, 8 * CH, 128), F32),
            pltpu.VMEM((AT_ONCE, 256, 256), BF16),
            pltpu.VMEM((AT_ONCE, 256, 256), BF16),
            pltpu.VMEM((AT_ONCE, 256, 256), F32),
            pltpu.VMEM((32 * CH, 128), F32),
        ],
    )(got, skip_gain)
    back = exchange(mixed)
    return call(gate_kernel, jax.ShapeDtypeStruct((512, 256), BF16))(
        back, key_branch, value_branch, gate_branch, skip_gain
    )


def solution(mesh):
    in_specs = (P("seq", "ch"), P("seq", "ch"), P("seq", "ch"), P("seq", "ch"), P("ch"))
    return jax.shard_map(
        on_device, mesh=mesh, in_specs=in_specs, out_specs=P("seq", "ch"), check_vma=False
    )
```

```python
import jax
import jax.numpy as jnp
from jax import lax
from jax.experimental import pallas as pl
from jax.experimental.pallas import tpu as pltpu
from jax.sharding import PartitionSpec as P

F32 = jnp.float32
BF16 = jnp.bfloat16
PARTS = 8
CH = 32
AT_ONCE = 8
PITCH = 40
VMEM = 48 * 1024 * 1024


def product_of(k, v):
    return (k.astype(F32) * v.astype(F32)).astype(BF16)


def pack_kernel(p_ref, f_ref, o_ref):
    p = p_ref[...].astype(F32)
    p = p.reshape(4, 8, 16, 256)
    p = jnp.stack([p[3 - a] for a in range(4)], 1).reshape(512, 256)
    f = f_ref[...].astype(F32)
    for half in range(2):
        for q in range(4):
            for at, x in ((0, p), (4, f)):
                block = x[128 * q : 128 * q + 128, 128 * half : 128 * half + 128]
                block = block.T.astype(BF16).reshape(4, CH, 128)
                o_ref[4 * half : 4 * half + 4, at + q] = block


def conv_kernel(r_ref, y_ref, g_s, v_s, a_s, b_s, o_s, y_s):
    lane = lax.broadcasted_iota(jnp.int32, (32, 128), 1)
    row = lax.broadcasted_iota(jnp.int32, (32, 128), 0)
    for s in range(PARTS):
        for q in range(4):
            g = 4 * s + q
            g_s[CH * g : CH * g + CH] = r_ref[s, 4 + q].astype(F32)
    for q in range(4):
        for j in range(4):
            first, second = [r_ref[s, q].astype(F32) for s in (2 * j + 1, 2 * j)]
            swapped = pltpu.roll(jnp.where(lane < 64, second, first), 64, 1)
            at = 2 * CH * q
            v_s[j, at : at + CH] = jnp.where(lane < 64, first, swapped)
            v_s[j, at + CH : at + 2 * CH] = jnp.where(lane < 64, swapped, second)
    stay_a = lane[:8] < 16 + 16 * row[:8]
    stay_b = lane[:16] >= row[:16]
    zero = jnp.zeros((8, 128), F32)

    def pair(a, b):
        return jnp.concatenate([a, b], 0).astype(BF16)

    def build(c, u):
        prev = jnp.zeros((16, 128), F32)
        for g in range(32):
            taps = jnp.broadcast_to(g_s[pl.ds(CH * g + c, 1), :], (16, 128))
            rot = pltpu.roll(taps, 0, 1, stride=1, stride_axis=0)
            at, half = 16 * (g % 16), 128 * (g // 16)
            b_s[u, at : at + 16, half : half + 128] = jnp.where(stay_b, rot, prev).astype(BF16)
            prev = rot
        for b in range(8):
            prev, w = zero, []
            for j in range(4):
                vals = jnp.broadcast_to(v_s[j, pl.ds(CH * b + c, 1), :], (8, 128))
                rot = pltpu.roll(vals, 16, 1, stride=16, stride_axis=0)
                w.append(jnp.where(stay_a, rot, prev))
                prev = rot
            lo, hi = slice(16 * b, 16 * b + 16), slice(128 + 16 * b, 144 + 16 * b)
            a_s[u, lo, :128] = pair(w[0], w[1])
            a_s[u, lo, 128:] = pair(zero, w[0])
            a_s[u, hi, :128] = pair(w[2], w[3])
            a_s[u, hi, 128:] = pair(w[1], w[2])

    def multiply(u):
        o_s[u] = jnp.dot(a_s[u], b_s[u], preferred_element_type=F32)

    def collect(c, u):
        here = jnp.zeros((32, 128), F32)
        late = jnp.zeros((32, 128), F32)
        for b in range(8):
            lo, hi = slice(16 * b, 16 * b + 16), slice(128 + 16 * b, 144 + 16 * b)
            r = jnp.concatenate([o_s[u, lo, :128], o_s[u, hi, :128] + o_s[u, lo, 128:]], 0)
            if b:
                r = pltpu.roll(r, 16 * b, 1)
                over = lane < 16 * b
                late = late + jnp.where(over, r, 0.0)
                r = jnp.where(over, 0.0, r)
            here = here + r
        late = jnp.where(row == 0, 0.0, pltpu.roll(late, 1, 0))
        y_s[pl.ds(c, 32, stride=PITCH), :] = here + late

    for u in range(AT_ONCE):
        build(u, u)
    for u in range(AT_ONCE):
        multiply(u)
    for u in range(AT_ONCE):
        build(AT_ONCE + u, u)

    def step(i, carry):
        for u in range(AT_ONCE):
            collect((i - 1) * AT_ONCE + u, u)
            multiply(u)
            build((i + 1) * AT_ONCE + u, u)
        return carry

    lax.fori_loop(1, CH // AT_ONCE - 1, step, 0)
    for u in range(AT_ONCE):
        collect(CH - 2 * AT_ONCE + u, u)
        multiply(u)
    for u in range(AT_ONCE):
        collect(CH - AT_ONCE + u, u)
    for s in range(PARTS):
        for q in range(4):
            at = PITCH * (4 * s + q)
            y_ref[s, q] = y_s[at : at + CH].astype(BF16)


def gate_kernel(y_ref, d_ref, g_ref, o_ref, o_s, sem):
    copies = []
    for q in range(4):
        pos = slice(128 * q, 128 * q + 128)
        for half in range(2):
            ch = slice(128 * half, 128 * half + 128)
            y = y_ref[4 * half : 4 * half + 4, q].reshape(128, 128).astype(F32).T
            out = g_ref[pos, ch].astype(F32) * (y + d_ref[pos, ch])
            o_s[pos, ch] = out.astype(BF16)
        copies.append(pltpu.make_async_copy(o_s.at[pos], o_ref.at[pos], sem.at[q]))
        copies[-1].start()
    for copy in copies:
        copy.wait()


def call(kernel, out, scratch=(), limit=VMEM, **more):
    return pl.pallas_call(
        kernel,
        out_shape=out,
        scratch_shapes=scratch,
        compiler_params=pltpu.CompilerParams(vmem_limit_bytes=limit),
        **more,
    )


def exchange(x):
    return lax.all_to_all(x, "seq", split_axis=0, concat_axis=0, tiled=True)


def on_device(key_branch, value_branch, gate_branch, conv_filter, skip_gain):
    product = product_of(key_branch, value_branch)
    direct = skip_gain[None, :] * product.astype(F32)
    sent = call(pack_kernel, jax.ShapeDtypeStruct((PARTS, 8, CH, 128), BF16))(
        product, conv_filter
    )
    got = exchange(sent)
    mixed = call(
        conv_kernel,
        jax.ShapeDtypeStruct((PARTS, 4, CH, 128), BF16),
        [
            pltpu.VMEM((32 * CH, 128), F32),
            pltpu.VMEM((4, 8 * CH, 128), F32),
            pltpu.VMEM((AT_ONCE, 256, 256), BF16),
            pltpu.VMEM((AT_ONCE, 256, 256), BF16),
            pltpu.VMEM((AT_ONCE, 256, 256), F32),
            pltpu.VMEM((32 * PITCH, 128), F32),
        ],
    )(got)
    back = exchange(mixed)
    return call(
        gate_kernel,
        jax.ShapeDtypeStruct((512, 256), BF16),
        [pltpu.VMEM((512, 256), BF16), pltpu.SemaphoreType.DMA((4,))],
        out_specs=pl.BlockSpec(memory_space=pl.ANY),
    )(back, direct, gate_branch)


def solution(mesh):
    in_specs = (P("seq", "ch"), P("seq", "ch"), P("seq", "ch"), P("seq", "ch"), P("ch"))
    return jax.shard_map(
        on_device, mesh=mesh, in_specs=in_specs, out_specs=P("seq", "ch"), check_vma=False
    )
```

```python
import jax
import jax.numpy as jnp
from jax import lax
from jax.experimental import pallas as pl
from jax.experimental.pallas import tpu as pltpu
from jax.sharding import PartitionSpec as P

F32 = jnp.float32
BF16 = jnp.bfloat16
PARTS = 8
CH = 32
ORDER = (0, 3, 1, 2)
AT_ONCE = 8
PITCH = 40
VMEM = 48 * 1024 * 1024


def pieces_of(refs):
    def piece(j, low, high):
        return refs[ORDER.index(j // 2)][j % 2, low:high]

    return piece


def pack_kernel(p_ref, f_ref, o_s):
    me = lax.axis_index("seq")
    p = p_ref[...].astype(F32)
    p = p.reshape(4, 8, 16, 256)
    p = jnp.stack([p[3 - a] for a in range(4)], 1).reshape(512, 256)
    f = f_ref[...].astype(F32)
    for half in range(2):
        for q in range(4):
            for at, x in ((0, p), (4, f)):
                block = x[128 * q : 128 * q + 128, 128 * half : 128 * half + 128]
                block = block.T.astype(BF16).reshape(4, CH, 128)
                for t in range(4):
                    o_s[lax.bitwise_xor(me, 4 * half + t), at + q] = block[t]


def conv_kernel(*refs):
    r_refs, (y_ref, g_s, v_s, a_s, b_s, o_s, y_s) = refs[:-7], refs[-7:]
    piece = pieces_of(r_refs)
    me = lax.axis_index("seq")
    odd = lax.rem(me, 2) == 1
    lane = lax.broadcasted_iota(jnp.int32, (32, 128), 1)
    row = lax.broadcasted_iota(jnp.int32, (32, 128), 0)
    for s in range(PARTS):
        at = pl.multiple_of(4 * CH * lax.bitwise_xor(me, s), 4 * CH)
        g_s[pl.ds(at, 4 * CH)] = piece(s, 4, 8).astype(F32).reshape(4 * CH, 128)
    for i in range(4):
        j = lax.div(lax.bitwise_xor(me, 2 * i), 2)
        mine, other = piece(2 * i, 0, 4).astype(F32), piece(2 * i + 1, 0, 4).astype(F32)
        firsts, seconds = jnp.where(odd, mine, other), jnp.where(odd, other, mine)
        for q in range(4):
            first, second = firsts[q], seconds[q]
            swapped = pltpu.roll(jnp.where(lane < 64, second, first), 64, 1)
            at = 2 * CH * q
            v_s[j, at : at + CH] = jnp.where(lane < 64, first, swapped)
            v_s[j, at + CH : at + 2 * CH] = jnp.where(lane < 64, swapped, second)
    stay_a = lane[:8] < 16 + 16 * row[:8]
    stay_b = lane[:16] >= row[:16]
    zero = jnp.zeros((8, 128), F32)

    def pair(a, b):
        return jnp.concatenate([a, b], 0).astype(BF16)

    def build(c, u):
        prev = jnp.zeros((16, 128), F32)
        for g in range(32):
            taps = jnp.broadcast_to(g_s[pl.ds(CH * g + c, 1), :], (16, 128))
            rot = pltpu.roll(taps, 0, 1, stride=1, stride_axis=0)
            at, half = 16 * (g % 16), 128 * (g // 16)
            b_s[u, at : at + 16, half : half + 128] = jnp.where(stay_b, rot, prev).astype(BF16)
            prev = rot
        for b in range(8):
            prev, w = zero, []
            for j in range(4):
                vals = jnp.broadcast_to(v_s[j, pl.ds(CH * b + c, 1), :], (8, 128))
                rot = pltpu.roll(vals, 16, 1, stride=16, stride_axis=0)
                w.append(jnp.where(stay_a, rot, prev))
                prev = rot
            lo, hi = slice(16 * b, 16 * b + 16), slice(128 + 16 * b, 144 + 16 * b)
            a_s[u, lo, :128] = pair(w[0], w[1])
            a_s[u, lo, 128:] = pair(zero, w[0])
            a_s[u, hi, :128] = pair(w[2], w[3])
            a_s[u, hi, 128:] = pair(w[1], w[2])

    def multiply(u):
        o_s[u] = jnp.dot(a_s[u], b_s[u], preferred_element_type=F32)

    def collect(c, u):
        here = jnp.zeros((32, 128), F32)
        late = jnp.zeros((32, 128), F32)
        for b in range(8):
            lo, hi = slice(16 * b, 16 * b + 16), slice(128 + 16 * b, 144 + 16 * b)
            r = jnp.concatenate([o_s[u, lo, :128], o_s[u, hi, :128] + o_s[u, lo, 128:]], 0)
            if b:
                r = pltpu.roll(r, 16 * b, 1)
                over = lane < 16 * b
                late = late + jnp.where(over, r, 0.0)
                r = jnp.where(over, 0.0, r)
            here = here + r
        late = jnp.where(row == 0, 0.0, pltpu.roll(late, 1, 0))
        y_s[pl.ds(c, 32, stride=PITCH), :] = here + late

    for u in range(AT_ONCE):
        build(u, u)
    for u in range(AT_ONCE):
        multiply(u)
    for u in range(AT_ONCE):
        build(AT_ONCE + u, u)

    def step(i, carry):
        for u in range(AT_ONCE):
            collect((i - 1) * AT_ONCE + u, u)
            multiply(u)
            build((i + 1) * AT_ONCE + u, u)
        return carry

    lax.fori_loop(1, CH // AT_ONCE - 1, step, 0)
    for u in range(AT_ONCE):
        collect(CH - 2 * AT_ONCE + u, u)
        multiply(u)
    for u in range(AT_ONCE):
        collect(CH - AT_ONCE + u, u)
    for s in range(PARTS):
        for q in range(4):
            at = PITCH * (4 * s + q)
            y_ref[lax.bitwise_xor(me, s), q] = y_s[at : at + CH].astype(BF16)


def gate_kernel(*refs):
    y_refs, (d_ref, g_ref, o_ref, y_s, o_s, sem) = refs[:-6], refs[-6:]
    piece = pieces_of(y_refs)
    me = lax.axis_index("seq")
    for s in range(PARTS):
        y_s[lax.bitwise_xor(me, s)] = piece(s, 0, 4)
    copies = []
    for q in range(4):
        pos = slice(128 * q, 128 * q + 128)
        for half in range(2):
            ch = slice(128 * half, 128 * half + 128)
            y = y_s[4 * half : 4 * half + 4, q].reshape(128, 128).astype(F32).T
            out = g_ref[pos, ch].astype(F32) * (y + d_ref[pos, ch])
            o_s[pos, ch] = out.astype(BF16)
        copies.append(pltpu.make_async_copy(o_s.at[pos], o_ref.at[pos], sem.at[q]))
        copies[-1].start()
    for copy in copies:
        copy.wait()


def call(kernel, out, scratch=(), limit=VMEM, **more):
    return pl.pallas_call(
        kernel,
        out_shape=out,
        scratch_shapes=scratch,
        compiler_params=pltpu.CompilerParams(vmem_limit_bytes=limit),
        **more,
    )


def swap(x, j):
    return lax.ppermute(x, "seq", [(i, i ^ j) for i in range(PARTS)])


def exchange(x):
    x = x.reshape(4, 2, *x.shape[1:])
    other = swap(x[:, 1], 1)
    pairs = jnp.stack([x[:, 0], other], 1)
    return [swap(pairs[i], 2 * i) if i else pairs[i] for i in ORDER]


def on_device(key_branch, value_branch, gate_branch, conv_filter, skip_gain):
    product = key_branch.astype(F32) * value_branch.astype(F32)
    product = lax.reduce_precision(product, 8, 7)
    direct = skip_gain[None, :] * product
    product = product.astype(BF16)
    sent = call(pack_kernel, jax.ShapeDtypeStruct((PARTS, 8, CH, 128), BF16))(
        product, conv_filter
    )
    got = exchange(sent)
    mixed = call(
        conv_kernel,
        jax.ShapeDtypeStruct((PARTS, 4, CH, 128), BF16),
        [
            pltpu.VMEM((32 * CH, 128), F32),
            pltpu.VMEM((4, 8 * CH, 128), F32),
            pltpu.VMEM((AT_ONCE, 256, 256), BF16),
            pltpu.VMEM((AT_ONCE, 256, 256), BF16),
            pltpu.VMEM((AT_ONCE, 256, 256), F32),
            pltpu.VMEM((32 * PITCH, 128), F32),
        ],
    )(*got)
    back = exchange(mixed)
    return call(
        gate_kernel,
        jax.ShapeDtypeStruct((512, 256), BF16),
        [
            pltpu.VMEM((PARTS, 4, CH, 128), BF16),
            pltpu.VMEM((512, 256), BF16),
            pltpu.SemaphoreType.DMA((4,)),
        ],
        out_specs=pl.BlockSpec(memory_space=pl.ANY),
    )(*back, direct, gate_branch)


def solution(mesh):
    in_specs = (P("seq", "ch"), P("seq", "ch"), P("seq", "ch"), P("seq", "ch"), P("ch"))
    return jax.shard_map(
        on_device, mesh=mesh, in_specs=in_specs, out_specs=P("seq", "ch"), check_vma=False
    )
```

```python
import jax
import jax.numpy as jnp
from jax import lax
from jax.experimental import pallas as pl
from jax.experimental.pallas import tpu as pltpu
from jax.sharding import PartitionSpec as P

F32 = jnp.float32
BF16 = jnp.bfloat16
PARTS = 8
CH = 32
ORDER = (0, 3, 1, 2)
AT_ONCE = 8
PITCH = 40
VMEM = 48 * 1024 * 1024


def pieces_of(refs):
    def piece(j, low, high):
        if len(refs) == 8:
            return refs[2 * (0, 3, 1, 2).index(j // 2) + j % 2][low:high]
        return refs[ORDER.index(j // 2)][j % 2, low:high]

    return piece


def pack_kernel(p_ref, f_ref, o_s):
    me = lax.axis_index("seq")
    p = p_ref[...].astype(F32)
    p = p.reshape(4, 8, 16, 256)
    p = jnp.stack([p[3 - a] for a in range(4)], 1).reshape(512, 256)
    f = f_ref[...].astype(F32)
    for half in range(2):
        for q in range(4):
            for at, x in ((0, p), (4, f)):
                block = x[128 * q : 128 * q + 128, 128 * half : 128 * half + 128]
                block = block.T.astype(BF16).reshape(4, CH, 128)
                for t in range(4):
                    o_s[lax.bitwise_xor(me, 4 * half + t), at + q] = block[t]


def conv_kernel(*refs):
    r_refs, (y_ref, g_s, v_s, a_s, b_s, o_s, y_s) = refs[:-7], refs[-7:]
    piece = pieces_of(r_refs)
    me = lax.axis_index("seq")
    odd = lax.rem(me, 2) == 1
    lane = lax.broadcasted_iota(jnp.int32, (32, 128), 1)
    row = lax.broadcasted_iota(jnp.int32, (32, 128), 0)
    for s in range(PARTS):
        at = pl.multiple_of(4 * CH * lax.bitwise_xor(me, s), 4 * CH)
        g_s[pl.ds(at, 4 * CH)] = piece(s, 4, 8).astype(F32).reshape(4 * CH, 128)
    for i in range(4):
        j = lax.div(lax.bitwise_xor(me, 2 * i), 2)
        mine, other = piece(2 * i, 0, 4).astype(F32), piece(2 * i + 1, 0, 4).astype(F32)
        firsts, seconds = jnp.where(odd, mine, other), jnp.where(odd, other, mine)
        for q in range(4):
            first, second = firsts[q], seconds[q]
            swapped = pltpu.roll(jnp.where(lane < 64, second, first), 64, 1)
            at = 2 * CH * q
            v_s[j, at : at + CH] = jnp.where(lane < 64, first, swapped)
            v_s[j, at + CH : at + 2 * CH] = jnp.where(lane < 64, swapped, second)
    stay_a = lane[:8] < 16 + 16 * row[:8]
    stay_b = lane[:16] >= row[:16]
    zero = jnp.zeros((8, 128), F32)

    def pair(a, b):
        return jnp.concatenate([a, b], 0).astype(BF16)

    def build(c, u):
        prev = jnp.zeros((16, 128), F32)
        for g in range(32):
            taps = jnp.broadcast_to(g_s[pl.ds(CH * g + c, 1), :], (16, 128))
            rot = pltpu.roll(taps, 0, 1, stride=1, stride_axis=0)
            at, half = 16 * (g % 16), 128 * (g // 16)
            b_s[u, at : at + 16, half : half + 128] = jnp.where(stay_b, rot, prev).astype(BF16)
            prev = rot
        for b in range(8):
            prev, w = zero, []
            for j in range(4):
                vals = jnp.broadcast_to(v_s[j, pl.ds(CH * b + c, 1), :], (8, 128))
                rot = pltpu.roll(vals, 16, 1, stride=16, stride_axis=0)
                w.append(jnp.where(stay_a, rot, prev))
                prev = rot
            lo, hi = slice(16 * b, 16 * b + 16), slice(128 + 16 * b, 144 + 16 * b)
            a_s[u, lo, :128] = pair(w[0], w[1])
            a_s[u, lo, 128:] = pair(zero, w[0])
            a_s[u, hi, :128] = pair(w[2], w[3])
            a_s[u, hi, 128:] = pair(w[1], w[2])

    def multiply(u):
        o_s[u] = jnp.dot(a_s[u], b_s[u], preferred_element_type=F32)

    def collect(c, u):
        here = jnp.zeros((32, 128), F32)
        late = jnp.zeros((32, 128), F32)
        for b in range(8):
            lo, hi = slice(16 * b, 16 * b + 16), slice(128 + 16 * b, 144 + 16 * b)
            r = jnp.concatenate([o_s[u, lo, :128], o_s[u, hi, :128] + o_s[u, lo, 128:]], 0)
            if b:
                r = pltpu.roll(r, 16 * b, 1)
                over = lane < 16 * b
                late = late + jnp.where(over, r, 0.0)
                r = jnp.where(over, 0.0, r)
            here = here + r
        late = jnp.where(row == 0, 0.0, pltpu.roll(late, 1, 0))
        y_s[pl.ds(c, 32, stride=PITCH), :] = here + late

    for u in range(AT_ONCE):
        build(u, u)
    for u in range(AT_ONCE):
        multiply(u)
    for u in range(AT_ONCE):
        build(AT_ONCE + u, u)

    def step(i, carry):
        for u in range(AT_ONCE):
            collect((i - 1) * AT_ONCE + u, u)
            multiply(u)
            build((i + 1) * AT_ONCE + u, u)
        return carry

    lax.fori_loop(1, CH // AT_ONCE - 1, step, 0)
    for u in range(AT_ONCE):
        collect(CH - 2 * AT_ONCE + u, u)
        multiply(u)
    for u in range(AT_ONCE):
        collect(CH - AT_ONCE + u, u)
    for s in range(PARTS):
        for q in range(4):
            at = PITCH * (4 * s + q)
            y_ref[lax.bitwise_xor(me, s), q] = y_s[at : at + CH].astype(BF16)


def gate_kernel(*refs):
    y_refs, (d_ref, g_ref, o_ref, y_s, o_s, sem) = refs[:-6], refs[-6:]
    piece = pieces_of(y_refs)
    me = lax.axis_index("seq")
    for s in range(PARTS):
        y_s[lax.bitwise_xor(me, s)] = piece(s, 0, 4)
    copies = []
    for q in range(4):
        pos = slice(128 * q, 128 * q + 128)
        for half in range(2):
            ch = slice(128 * half, 128 * half + 128)
            y = y_s[4 * half : 4 * half + 4, q].reshape(128, 128).astype(F32).T
            out = g_ref[pos, ch].astype(F32) * (y + d_ref[pos, ch])
            o_s[pos, ch] = out.astype(BF16)
        copies.append(pltpu.make_async_copy(o_s.at[pos], o_ref.at[pos], sem.at[q]))
        copies[-1].start()
    for copy in copies:
        copy.wait()


def call(kernel, out, scratch=(), limit=VMEM, **more):
    return pl.pallas_call(
        kernel,
        out_shape=out,
        scratch_shapes=scratch,
        compiler_params=pltpu.CompilerParams(vmem_limit_bytes=limit),
        **more,
    )


def swap(x, j):
    return lax.ppermute(x, "seq", [(i, i ^ j) for i in range(PARTS)])


def exchange(x):
    x = x.reshape(4, 2, *x.shape[1:])
    other = swap(x[:, 1], 1)
    pairs = jnp.stack([x[:, 0], other], 1)
    return [swap(pairs[i], 2 * i) if i else pairs[i] for i in ORDER]


def z_first(x):
    x = x.reshape(4, 2, *x.shape[1:])
    out = []
    for i in (0, 3, 1, 2):
        pair = swap(x[i], 2 * i) if i else x[0]
        out += [pair[0], swap(pair[1], 1)]
    return out


def on_device(key_branch, value_branch, gate_branch, conv_filter, skip_gain):
    product = key_branch.astype(F32) * value_branch.astype(F32)
    product = lax.reduce_precision(product, 8, 7)
    direct = skip_gain[None, :] * product
    product = product.astype(BF16)
    sent = call(pack_kernel, jax.ShapeDtypeStruct((PARTS, 8, CH, 128), BF16))(
        product, conv_filter
    )
    got = z_first(sent)
    mixed = call(
        conv_kernel,
        jax.ShapeDtypeStruct((PARTS, 4, CH, 128), BF16),
        [
            pltpu.VMEM((32 * CH, 128), F32),
            pltpu.VMEM((4, 8 * CH, 128), F32),
            pltpu.VMEM((AT_ONCE, 256, 256), BF16),
            pltpu.VMEM((AT_ONCE, 256, 256), BF16),
            pltpu.VMEM((AT_ONCE, 256, 256), F32),
            pltpu.VMEM((32 * PITCH, 128), F32),
        ],
    )(*got)
    back = exchange(mixed)
    return call(
        gate_kernel,
        jax.ShapeDtypeStruct((512, 256), BF16),
        [
            pltpu.VMEM((PARTS, 4, CH, 128), BF16),
            pltpu.VMEM((512, 256), BF16),
            pltpu.SemaphoreType.DMA((4,)),
        ],
        out_specs=pl.BlockSpec(memory_space=pl.ANY),
    )(*back, direct, gate_branch)


def solution(mesh):
    in_specs = (P("seq", "ch"), P("seq", "ch"), P("seq", "ch"), P("seq", "ch"), P("ch"))
    return jax.shard_map(
        on_device, mesh=mesh, in_specs=in_specs, out_specs=P("seq", "ch"), check_vma=False
    )
```

```python
import jax
import jax.numpy as jnp
from jax import lax
from jax.experimental import pallas as pl
from jax.experimental.pallas import tpu as pltpu
from jax.sharding import PartitionSpec as P

F32 = jnp.float32
BF16 = jnp.bfloat16
PARTS = 8
CH = 32
ORDER = (0, 3, 1, 2)
AT_ONCE = 8
SPREAD_AT_ONCE = 32
PITCH = 40
VMEM = 24 * 1024 * 1024


def pieces_of(refs):
    def piece(j, low, high):
        return refs[ORDER.index(j // 2)][j % 2, low:high]

    return piece


def pack_kernel(p_ref, f_ref, o_s):
    me = lax.axis_index("seq")
    p = p_ref[...].astype(F32)
    p = p.reshape(4, 8, 16, 256)
    p = jnp.stack([p[3 - a] for a in range(4)], 1).reshape(512, 256)
    f = f_ref[...].astype(F32)
    for half in range(2):
        for q in range(4):
            for at, x in ((0, p), (4, f)):
                block = x[128 * q : 128 * q + 128, 128 * half : 128 * half + 128]
                block = block.T.astype(BF16).reshape(4, CH, 128)
                for t in range(4):
                    o_s[lax.bitwise_xor(me, 4 * half + t), at + q] = block[t]


def spread_kernel(pair_ref, t_ref, w_ref, g_s, v_s):
    odd = lax.rem(lax.axis_index("seq"), 2)
    lane = lax.broadcasted_iota(jnp.int32, (32, 128), 1)
    row = lax.broadcasted_iota(jnp.int32, (32, 128), 0)
    for j, at in ((0, odd), (1, 1 - odd)):
        at = pl.multiple_of(4 * CH * at, 4 * CH)
        g_s[pl.ds(at, 4 * CH)] = pair_ref[j, 4:8].astype(F32).reshape(4 * CH, 128)
    mine, other = pair_ref[0, 0:4].astype(F32), pair_ref[1, 0:4].astype(F32)
    firsts, seconds = jnp.where(odd == 1, mine, other), jnp.where(odd == 1, other, mine)
    for q in range(4):
        first, second = firsts[q], seconds[q]
        swapped = pltpu.roll(jnp.where(lane < 64, second, first), 64, 1)
        at = 2 * CH * q
        v_s[at : at + CH] = jnp.where(lane < 64, first, swapped)
        v_s[at + CH : at + 2 * CH] = jnp.where(lane < 64, swapped, second)
    stay_a = lane[:16] < 16 + 16 * (row[:16] % 8)
    stay_b = lane[:16] >= row[:16]

    def spread(c):
        prev = jnp.zeros((16, 128), F32)
        for g in range(8):
            taps = jnp.broadcast_to(g_s[pl.ds(CH * g + c, 1), :], (16, 128))
            rot = pltpu.roll(taps, 0, 1, stride=1, stride_axis=0)
            t_ref[c, 16 * g : 16 * g + 16] = jnp.where(stay_b, rot, prev).astype(BF16)
            prev = rot
        t_ref[c, 128:144] = jnp.where(stay_b, 0.0, prev).astype(BF16)
        for b in range(0, 8, 2):
            rots = []
            for j in range(2):
                vals = jnp.broadcast_to(v_s[pl.ds(CH * (b + j) + c, 1), :], (8, 128))
                rots.append(pltpu.roll(vals, 16, 1, stride=16, stride_axis=0))
            rot = jnp.concatenate(rots, 0)
            w_ref[c, 8 * b : 8 * b + 16] = jnp.where(stay_a, rot, 0.0).astype(BF16)
            w_ref[c, 64 + 8 * b : 80 + 8 * b] = jnp.where(stay_a, 0.0, rot).astype(BF16)

    def step(i, carry):
        for u in range(SPREAD_AT_ONCE):
            spread(i * SPREAD_AT_ONCE + u)
        return carry

    lax.fori_loop(0, CH // SPREAD_AT_ONCE, step, 0)


def conv_kernel(*refs):
    ts, ws, (y_ref, o_s, y_s) = refs[:4], refs[4:8], refs[8:]
    me = lax.axis_index("seq")
    z = lax.div(me, 2)
    for at in range(4):
        order = [at ^ chip for chip in range(4)]

        @pl.when(z == at)
        def _(order=order):
            convolve([ts[i] for i in order], [ws[i] for i in order], o_s, y_s)

    for s in range(PARTS):
        for q in range(4):
            at = PITCH * (4 * s + q)
            y_ref[lax.bitwise_xor(me, s), q] = y_s[at : at + CH].astype(BF16)


def convolve(ts, ws, o_s, y_s):
    lane = lax.broadcasted_iota(jnp.int32, (32, 128), 1)
    row = lax.broadcasted_iota(jnp.int32, (32, 128), 0)

    def multiply(c, u):
        right = [ts[0][c, 0:128]]
        for j in range(1, 4):
            first = ts[j][c, 0:16] + ts[j - 1][c, 128:144]
            right.append(jnp.concatenate([first, ts[j][c, 16:128]], 0))
        right = jnp.concatenate(
            [jnp.concatenate(right[0:2], 0), jnp.concatenate(right[2:4], 0)], 1
        )
        w = [ws[0][c, 0:64]] + [ws[j][c, 0:64] + ws[j - 1][c, 64:128] for j in range(1, 4)]
        zero = jnp.zeros((64, 128), BF16)
        left = jnp.concatenate(
            [jnp.concatenate([w[j], w[j - 1] if j else zero], 1) for j in range(4)], 0
        )
        o_s[u] = jnp.dot(left, right, preferred_element_type=F32)

    def collect(c, u):
        here = jnp.zeros((32, 128), F32)
        late = jnp.zeros((32, 128), F32)
        for b in range(8):
            r = []
            for j in range(4):
                part = o_s[u, 64 * j + 8 * b : 64 * j + 8 * b + 8, :128]
                if j >= 2:
                    at = 64 * (j - 2) + 8 * b
                    part = part + o_s[u, at : at + 8, 128:]
                r.append(part)
            r = jnp.concatenate(r, 0)
            if b:
                r = pltpu.roll(r, 16 * b, 1)
                over = lane < 16 * b
                late = late + jnp.where(over, r, 0.0)
                r = jnp.where(over, 0.0, r)
            here = here + r
        late = jnp.where(row == 0, 0.0, pltpu.roll(late, 1, 0))
        y_s[pl.ds(c, 32, stride=PITCH), :] = here + late

    for u in range(AT_ONCE):
        multiply(u, u)

    def step(i, carry):
        for u in range(AT_ONCE):
            collect((i - 1) * AT_ONCE + u, u)
            multiply(i * AT_ONCE + u, u)
        return carry

    lax.fori_loop(1, CH // AT_ONCE, step, 0)
    for u in range(AT_ONCE):
        collect(CH - AT_ONCE + u, u)


def gate_kernel(*refs):
    y_refs, (d_ref, g_ref, o_ref, y_s, o_s, sem) = refs[:-6], refs[-6:]
    piece = pieces_of(y_refs)
    me = lax.axis_index("seq")
    for s in range(PARTS):
        y_s[lax.bitwise_xor(me, s)] = piece(s, 0, 4)
    copies = []
    for q in range(4):
        pos = slice(128 * q, 128 * q + 128)
        for half in range(2):
            ch = slice(128 * half, 128 * half + 128)
            y = y_s[4 * half : 4 * half + 4, q].reshape(128, 128).astype(F32).T
            out = g_ref[pos, ch].astype(F32) * (y + d_ref[pos, ch])
            o_s[pos, ch] = out.astype(BF16)
        copies.append(pltpu.make_async_copy(o_s.at[pos], o_ref.at[pos], sem.at[q]))
        copies[-1].start()
    for copy in copies:
        copy.wait()


def call(kernel, out, scratch=(), limit=VMEM, **more):
    return pl.pallas_call(
        kernel,
        out_shape=out,
        scratch_shapes=scratch,
        compiler_params=pltpu.CompilerParams(vmem_limit_bytes=limit),
        **more,
    )


def swap(x, j):
    return lax.ppermute(x, "seq", [(i, i ^ j) for i in range(PARTS)])


def exchange(x):
    x = x.reshape(4, 2, *x.shape[1:])
    other = swap(x[:, 1], 1)
    pairs = jnp.stack([x[:, 0], other], 1)
    return [swap(pairs[i], 2 * i) if i else pairs[i] for i in ORDER]


def on_device(key_branch, value_branch, gate_branch, conv_filter, skip_gain):
    product = key_branch.astype(F32) * value_branch.astype(F32)
    product = lax.reduce_precision(product, 8, 7)
    direct = skip_gain[None, :] * product
    product = product.astype(BF16)
    sent = call(pack_kernel, jax.ShapeDtypeStruct((PARTS, 8, CH, 128), BF16))(
        product, conv_filter
    )
    pairs = dict(zip(ORDER, exchange(sent)))
    tiles = [None] * 4
    for last, i in ((None, 0), (0, 2), (2, 3), (3, 1)):
        pair = pairs[i]
        if last is not None:
            pair, tiles[last] = lax.optimization_barrier((pair, tiles[last]))
        tiles[i] = call(
            spread_kernel,
            [
                jax.ShapeDtypeStruct((CH, 144, 128), BF16),
                jax.ShapeDtypeStruct((CH, 128, 128), BF16),
            ],
            [pltpu.VMEM((8 * CH, 128), F32)] * 2,
            cost_estimate=pl.CostEstimate(flops=10**9, bytes_accessed=10**7, transcendentals=0),
        )(pair)
    mixed = call(
        conv_kernel,
        jax.ShapeDtypeStruct((PARTS, 4, CH, 128), BF16),
        [
            pltpu.VMEM((AT_ONCE, 256, 256), F32),
            pltpu.VMEM((32 * PITCH, 128), F32),
        ],
    )(*[t for t, _ in tiles], *[w for _, w in tiles])
    back = exchange(mixed)
    return call(
        gate_kernel,
        jax.ShapeDtypeStruct((512, 256), BF16),
        [
            pltpu.VMEM((PARTS, 4, CH, 128), BF16),
            pltpu.VMEM((512, 256), BF16),
            pltpu.SemaphoreType.DMA((4,)),
        ],
        out_specs=pl.BlockSpec(memory_space=pl.ANY),
    )(*back, direct, gate_branch)


def solution(mesh):
    in_specs = (P("seq", "ch"), P("seq", "ch"), P("seq", "ch"), P("seq", "ch"), P("ch"))
    return jax.shard_map(
        on_device, mesh=mesh, in_specs=in_specs, out_specs=P("seq", "ch"), check_vma=False
    )
```

```python
import jax
import jax.numpy as jnp
from jax import lax
from jax.experimental import pallas as pl
from jax.experimental.pallas import tpu as pltpu
from jax.sharding import PartitionSpec as P

F32 = jnp.float32
BF16 = jnp.bfloat16
PARTS = 8
CH = 32
ORDER = (0, 3, 1, 2)
AT_ONCE = 8
BEHIND = 4
SPREAD_AT_ONCE = 32
PITCH = 40
VMEM = 24 * 1024 * 1024


def pieces_of(refs):
    def piece(j, low, high):
        return refs[ORDER.index(j // 2)][j % 2, low:high]

    return piece


def pack_kernel(p_ref, f_ref, o_s):
    me = lax.axis_index("seq")
    p = p_ref[...].astype(F32)
    p = p.reshape(4, 8, 16, 256)
    p = jnp.stack([p[3 - a] for a in range(4)], 1).reshape(512, 256)
    f = f_ref[...].astype(F32)
    for half in range(2):
        for q in range(4):
            for at, x in ((0, p), (4, f)):
                block = x[128 * q : 128 * q + 128, 128 * half : 128 * half + 128]
                block = block.T.astype(BF16).reshape(4, CH, 128)
                for t in range(4):
                    o_s[lax.bitwise_xor(me, 4 * half + t), at + q] = block[t]


def spread_kernel(pair_ref, t_ref, w_ref, g_s, v_s):
    odd = lax.rem(lax.axis_index("seq"), 2)
    lane = lax.broadcasted_iota(jnp.int32, (32, 128), 1)
    row = lax.broadcasted_iota(jnp.int32, (32, 128), 0)
    for j, at in ((0, odd), (1, 1 - odd)):
        at = pl.multiple_of(4 * CH * at, 4 * CH)
        g_s[pl.ds(at, 4 * CH)] = pair_ref[j, 4:8].astype(F32).reshape(4 * CH, 128)
    mine, other = pair_ref[0, 0:4].astype(F32), pair_ref[1, 0:4].astype(F32)
    firsts, seconds = jnp.where(odd == 1, mine, other), jnp.where(odd == 1, other, mine)
    for q in range(4):
        first, second = firsts[q], seconds[q]
        swapped = pltpu.roll(jnp.where(lane < 64, second, first), 64, 1)
        at = 2 * CH * q
        v_s[at : at + CH] = jnp.where(lane < 64, first, swapped)
        v_s[at + CH : at + 2 * CH] = jnp.where(lane < 64, swapped, second)
    stay_a = lane[:16] < 16 + 16 * (row[:16] % 8)
    stay_b = lane[:16] >= row[:16]

    def spread(c):
        prev = jnp.zeros((16, 128), F32)
        for g in range(8):
            taps = jnp.broadcast_to(g_s[pl.ds(CH * g + c, 1), :], (16, 128))
            rot = pltpu.roll(taps, 0, 1, stride=1, stride_axis=0)
            t_ref[c, 16 * g : 16 * g + 16] = jnp.where(stay_b, rot, prev).astype(BF16)
            prev = rot
        t_ref[c, 128:144] = jnp.where(stay_b, 0.0, prev).astype(BF16)
        for b in range(0, 8, 2):
            rots = []
            for j in range(2):
                vals = jnp.broadcast_to(v_s[pl.ds(CH * (b + j) + c, 1), :], (8, 128))
                rots.append(pltpu.roll(vals, 16, 1, stride=16, stride_axis=0))
            rot = jnp.concatenate(rots, 0)
            w_ref[c, 8 * b : 8 * b + 16] = jnp.where(stay_a, rot, 0.0).astype(BF16)
            w_ref[c, 64 + 8 * b : 80 + 8 * b] = jnp.where(stay_a, 0.0, rot).astype(BF16)

    def step(i, carry):
        for u in range(SPREAD_AT_ONCE):
            spread(i * SPREAD_AT_ONCE + u)
        return carry

    lax.fori_loop(0, CH // SPREAD_AT_ONCE, step, 0)


def conv_kernel(*refs):
    ts, ws, (y_ref, o_s, y_s) = refs[:4], refs[4:8], refs[8:]
    me = lax.axis_index("seq")
    z = lax.div(me, 2)
    for at in range(4):
        order = [at ^ chip for chip in range(4)]

        @pl.when(z == at)
        def _(order=order):
            convolve([ts[i] for i in order], [ws[i] for i in order], o_s, y_s)

    for s in range(PARTS):
        for q in range(4):
            at = PITCH * (4 * s + q)
            y_ref[lax.bitwise_xor(me, s), q] = y_s[at : at + CH].astype(BF16)


def convolve(ts, ws, o_s, y_s):
    lane = lax.broadcasted_iota(jnp.int32, (32, 128), 1)
    row = lax.broadcasted_iota(jnp.int32, (32, 128), 0)

    def multiply(c, u):
        right = [ts[0][c, 0:128]]
        for j in range(1, 4):
            first = ts[j][c, 0:16] + ts[j - 1][c, 128:144]
            right.append(jnp.concatenate([first, ts[j][c, 16:128]], 0))
        right = jnp.concatenate(
            [jnp.concatenate(right[0:2], 0), jnp.concatenate(right[2:4], 0)], 1
        )
        w = [ws[0][c, 0:64]] + [ws[j][c, 0:64] + ws[j - 1][c, 64:128] for j in range(1, 4)]
        zero = jnp.zeros((64, 128), BF16)
        left = jnp.concatenate(
            [jnp.concatenate([w[j], w[j - 1] if j else zero], 1) for j in range(4)], 0
        )
        o_s[u] = jnp.dot(left, right, preferred_element_type=F32)

    def collect(c, u):
        here = jnp.zeros((32, 128), F32)
        late = jnp.zeros((32, 128), F32)
        for b in range(8):
            r = []
            for j in range(4):
                part = o_s[u, 64 * j + 8 * b : 64 * j + 8 * b + 8, :128]
                if j >= 2:
                    at = 64 * (j - 2) + 8 * b
                    part = part + o_s[u, at : at + 8, 128:]
                r.append(part)
            r = jnp.concatenate(r, 0)
            if b:
                r = pltpu.roll(r, 16 * b, 1)
                over = lane < 16 * b
                late = late + jnp.where(over, r, 0.0)
                r = jnp.where(over, 0.0, r)
            here = here + r
        late = jnp.where(row == 0, 0.0, pltpu.roll(late, 1, 0))
        y_s[pl.ds(c, 32, stride=PITCH), :] = here + late

    for c in range(CH):
        multiply(c, c % AT_ONCE)
        if c >= BEHIND:
            collect(c - BEHIND, (c - BEHIND) % AT_ONCE)
    for c in range(CH - BEHIND, CH):
        collect(c, c % AT_ONCE)


def gate_kernel(*refs):
    y_refs, (d_ref, g_ref, o_ref, y_s, o_s, sem) = refs[:-6], refs[-6:]
    piece = pieces_of(y_refs)
    me = lax.axis_index("seq")
    for s in range(PARTS):
        y_s[lax.bitwise_xor(me, s)] = piece(s, 0, 4)
    copies = []
    for q in range(4):
        pos = slice(128 * q, 128 * q + 128)
        for half in range(2):
            ch = slice(128 * half, 128 * half + 128)
            y = y_s[4 * half : 4 * half + 4, q].reshape(128, 128).astype(F32).T
            out = g_ref[pos, ch].astype(F32) * (y + d_ref[pos, ch])
            o_s[pos, ch] = out.astype(BF16)
        copies.append(pltpu.make_async_copy(o_s.at[pos], o_ref.at[pos], sem.at[q]))
        copies[-1].start()
    for copy in copies:
        copy.wait()


def call(kernel, out, scratch=(), limit=VMEM, **more):
    return pl.pallas_call(
        kernel,
        out_shape=out,
        scratch_shapes=scratch,
        compiler_params=pltpu.CompilerParams(vmem_limit_bytes=limit),
        **more,
    )


def swap(x, j):
    return lax.ppermute(x, "seq", [(i, i ^ j) for i in range(PARTS)])


def exchange(x):
    x = x.reshape(4, 2, *x.shape[1:])
    other = swap(x[:, 1], 1)
    pairs = jnp.stack([x[:, 0], other], 1)
    return [swap(pairs[i], 2 * i) if i else pairs[i] for i in ORDER]


def on_device(key_branch, value_branch, gate_branch, conv_filter, skip_gain):
    product = key_branch.astype(F32) * value_branch.astype(F32)
    product = lax.reduce_precision(product, 8, 7)
    direct = skip_gain[None, :] * product
    product = product.astype(BF16)
    sent = call(pack_kernel, jax.ShapeDtypeStruct((PARTS, 8, CH, 128), BF16))(
        product, conv_filter
    )
    pairs = dict(zip(ORDER, exchange(sent)))
    tiles = [None] * 4
    for last, i in ((None, 0), (0, 2), (2, 3), (3, 1)):
        pair = pairs[i]
        if last is not None:
            pair, tiles[last] = lax.optimization_barrier((pair, tiles[last]))
        tiles[i] = call(
            spread_kernel,
            [
                jax.ShapeDtypeStruct((CH, 144, 128), BF16),
                jax.ShapeDtypeStruct((CH, 128, 128), BF16),
            ],
            [pltpu.VMEM((8 * CH, 128), F32)] * 2,
            cost_estimate=pl.CostEstimate(flops=10**9, bytes_accessed=10**7, transcendentals=0),
        )(pair)
    mixed = call(
        conv_kernel,
        jax.ShapeDtypeStruct((PARTS, 4, CH, 128), BF16),
        [
            pltpu.VMEM((AT_ONCE, 256, 256), F32),
            pltpu.VMEM((32 * PITCH, 128), F32),
        ],
    )(*[t for t, _ in tiles], *[w for _, w in tiles])
    back = exchange(mixed)
    return call(
        gate_kernel,
        jax.ShapeDtypeStruct((512, 256), BF16),
        [
            pltpu.VMEM((PARTS, 4, CH, 128), BF16),
            pltpu.VMEM((512, 256), BF16),
            pltpu.SemaphoreType.DMA((4,)),
        ],
        out_specs=pl.BlockSpec(memory_space=pl.ANY),
    )(*back, direct, gate_branch)


def solution(mesh):
    in_specs = (P("seq", "ch"), P("seq", "ch"), P("seq", "ch"), P("seq", "ch"), P("ch"))
    return jax.shard_map(
        on_device, mesh=mesh, in_specs=in_specs, out_specs=P("seq", "ch"), check_vma=False
    )
```

```python
import jax
import jax.numpy as jnp
from jax import lax
from jax.experimental import pallas as pl
from jax.experimental.pallas import tpu as pltpu
from jax.sharding import PartitionSpec as P

F32 = jnp.float32
BF16 = jnp.bfloat16
PARTS = 8
CH = 32
AT_ONCE = 8
BEHIND = 4
SPREAD_AT_ONCE = 32
PITCH = 40
VMEM = 24 * 1024 * 1024


def slot_of(j):
    return lax.select(j >= 6, j, lax.rem(j + 2, 6))


def pack_kernel(p_ref, f_ref, o_s):
    me = lax.axis_index("seq")
    p = p_ref[...].astype(F32)
    p = p.reshape(4, 8, 16, 256)
    p = jnp.stack([p[3 - a] for a in range(4)], 1).reshape(512, 256)
    f = f_ref[...].astype(F32)
    for half in range(2):
        for q in range(4):
            for at, x in ((0, p), (4, f)):
                block = x[128 * q : 128 * q + 128, 128 * half : 128 * half + 128]
                block = block.T.astype(BF16).reshape(4, CH, 128)
                for t in range(4):
                    o_s[lax.bitwise_xor(me, 4 * half + t), at + q] = block[t]


def both(refs):
    return refs if len(refs) == 2 else (refs[0].at[0], refs[0].at[1])


def spread_kernel(*refs):
    pair, (t_ref, w_ref, g_s, v_s) = both(refs[:-4]), refs[-4:]
    odd = lax.rem(lax.axis_index("seq"), 2)
    lane = lax.broadcasted_iota(jnp.int32, (32, 128), 1)
    row = lax.broadcasted_iota(jnp.int32, (32, 128), 0)
    for j, at in ((0, odd), (1, 1 - odd)):
        at = pl.multiple_of(4 * CH * at, 4 * CH)
        g_s[pl.ds(at, 4 * CH)] = pair[j][4:8].astype(F32).reshape(4 * CH, 128)
    mine, other = pair[0][0:4].astype(F32), pair[1][0:4].astype(F32)
    firsts, seconds = jnp.where(odd == 1, mine, other), jnp.where(odd == 1, other, mine)
    for q in range(4):
        first, second = firsts[q], seconds[q]
        swapped = pltpu.roll(jnp.where(lane < 64, second, first), 64, 1)
        at = 2 * CH * q
        v_s[at : at + CH] = jnp.where(lane < 64, first, swapped)
        v_s[at + CH : at + 2 * CH] = jnp.where(lane < 64, swapped, second)
    stay_a = lane[:16] < 16 + 16 * (row[:16] % 8)
    stay_b = lane[:16] >= row[:16]

    def spread(c):
        prev = jnp.zeros((16, 128), F32)
        for g in range(8):
            taps = jnp.broadcast_to(g_s[pl.ds(CH * g + c, 1), :], (16, 128))
            rot = pltpu.roll(taps, 0, 1, stride=1, stride_axis=0)
            t_ref[c, 16 * g : 16 * g + 16] = jnp.where(stay_b, rot, prev).astype(BF16)
            prev = rot
        t_ref[c, 128:144] = jnp.where(stay_b, 0.0, prev).astype(BF16)
        for b in range(0, 8, 2):
            rots = []
            for j in range(2):
                vals = jnp.broadcast_to(v_s[pl.ds(CH * (b + j) + c, 1), :], (8, 128))
                rots.append(pltpu.roll(vals, 16, 1, stride=16, stride_axis=0))
            rot = jnp.concatenate(rots, 0)
            w_ref[c, 8 * b : 8 * b + 16] = jnp.where(stay_a, rot, 0.0).astype(BF16)
            w_ref[c, 64 + 8 * b : 80 + 8 * b] = jnp.where(stay_a, 0.0, rot).astype(BF16)

    def step(i, carry):
        for u in range(SPREAD_AT_ONCE):
            spread(i * SPREAD_AT_ONCE + u)
        return carry

    lax.fori_loop(0, CH // SPREAD_AT_ONCE, step, 0)


def conv_kernel(*refs):
    ts, ws, (y_ref, o_s, y_s) = refs[:4], refs[4:8], refs[8:]
    me = lax.axis_index("seq")
    z = lax.div(me, 2)
    for at in range(4):
        order = [at ^ chip for chip in range(4)]

        @pl.when(z == at)
        def _(order=order):
            convolve([ts[i] for i in order], [ws[i] for i in order], o_s, y_s)

    for s in range(PARTS):
        for q in range(4):
            at = PITCH * (4 * s + q)
            y_ref[slot_of(lax.bitwise_xor(me, s)), q] = y_s[at : at + CH].astype(BF16)


def convolve(ts, ws, o_s, y_s):
    lane = lax.broadcasted_iota(jnp.int32, (32, 128), 1)
    row = lax.broadcasted_iota(jnp.int32, (32, 128), 0)

    def multiply(c, u):
        right = [ts[0][c, 0:128]]
        for j in range(1, 4):
            first = ts[j][c, 0:16] + ts[j - 1][c, 128:144]
            right.append(jnp.concatenate([first, ts[j][c, 16:128]], 0))
        right = jnp.concatenate(
            [jnp.concatenate(right[0:2], 0), jnp.concatenate(right[2:4], 0)], 1
        )
        w = [ws[0][c, 0:64]] + [ws[j][c, 0:64] + ws[j - 1][c, 64:128] for j in range(1, 4)]
        zero = jnp.zeros((64, 128), BF16)
        left = jnp.concatenate(
            [jnp.concatenate([w[j], w[j - 1] if j else zero], 1) for j in range(4)], 0
        )
        o_s[u] = jnp.dot(left, right, preferred_element_type=F32)

    def collect(c, u):
        here = jnp.zeros((32, 128), F32)
        late = jnp.zeros((32, 128), F32)
        for b in range(8):
            r = []
            for j in range(4):
                part = o_s[u, 64 * j + 8 * b : 64 * j + 8 * b + 8, :128]
                if j >= 2:
                    at = 64 * (j - 2) + 8 * b
                    part = part + o_s[u, at : at + 8, 128:]
                r.append(part)
            r = jnp.concatenate(r, 0)
            if b:
                r = pltpu.roll(r, 16 * b, 1)
                over = lane < 16 * b
                late = late + jnp.where(over, r, 0.0)
                r = jnp.where(over, 0.0, r)
            here = here + r
        late = jnp.where(row == 0, 0.0, pltpu.roll(late, 1, 0))
        y_s[pl.ds(c, 32, stride=PITCH), :] = here + late

    for c in range(CH):
        multiply(c, c % AT_ONCE)
        if c >= BEHIND:
            collect(c - BEHIND, (c - BEHIND) % AT_ONCE)
    for c in range(CH - BEHIND, CH):
        collect(c, c % AT_ONCE)


def gate_kernel(*refs):
    y_refs, (d_ref, g_ref, o_ref, y_s, o_s, sem) = refs[:-6], refs[-6:]
    me = lax.axis_index("seq")
    pairs = [both(y_refs[i : i + n]) for i, n in ((0, 1), (1, 1), (2, 2), (4, 1))]
    for s in range(PARTS):
        y_s[lax.bitwise_xor(me, s)] = pairs[s // 2][s % 2][...]
    copies = []
    for q in range(4):
        pos = slice(128 * q, 128 * q + 128)
        for half in range(2):
            ch = slice(128 * half, 128 * half + 128)
            y = y_s[4 * half : 4 * half + 4, q].reshape(128, 128).astype(F32).T
            out = g_ref[pos, ch].astype(F32) * (y + d_ref[pos, ch])
            o_s[pos, ch] = out.astype(BF16)
        copies.append(pltpu.make_async_copy(o_s.at[pos], o_ref.at[pos], sem.at[q]))
        copies[-1].start()
    for copy in copies:
        copy.wait()


def call(kernel, out, scratch=(), limit=VMEM, **more):
    return pl.pallas_call(
        kernel,
        out_shape=out,
        scratch_shapes=scratch,
        compiler_params=pltpu.CompilerParams(vmem_limit_bytes=limit),
        **more,
    )


def swap(x, j):
    return lax.ppermute(x, "seq", [(i, i ^ j) for i in range(PARTS)])


def exchange(x):
    x = x.reshape(4, 2, *x.shape[1:])
    pairs = jnp.stack([x[:, 0], swap(x[:, 1], 1)], 1)
    return [(pairs[0],)] + [(swap(pairs[i], 2 * i),) for i in range(1, 4)]


def exchange_far_first(x):
    x = x.reshape(4, 2, *x.shape[1:])
    far = swap(x[0], 4)
    other = swap(x[1:, 1], 1)
    near = jnp.stack([x[1:, 0], other], 1)
    return [
        (near[0],),
        (swap(near[1], 2),),
        (far[0], swap(far[1], 1)),
        (swap(near[2], 6),),
    ]


def on_device(key_branch, value_branch, gate_branch, conv_filter, skip_gain):
    product = key_branch.astype(F32) * value_branch.astype(F32)
    product = lax.reduce_precision(product, 8, 7)
    direct = skip_gain[None, :] * product
    product = product.astype(BF16)
    sent = call(pack_kernel, jax.ShapeDtypeStruct((PARTS, 8, CH, 128), BF16))(
        product, conv_filter
    )
    pairs = exchange(sent)
    tiles = [None] * 4
    for last, i in ((None, 0), (0, 2), (2, 3), (3, 1)):
        pair = pairs[i]
        if last is not None:
            pair, tiles[last] = lax.optimization_barrier((pair, tiles[last]))
        tiles[i] = call(
            spread_kernel,
            [
                jax.ShapeDtypeStruct((CH, 144, 128), BF16),
                jax.ShapeDtypeStruct((CH, 128, 128), BF16),
            ],
            [pltpu.VMEM((8 * CH, 128), F32)] * 2,
            cost_estimate=pl.CostEstimate(flops=10**9, bytes_accessed=10**7, transcendentals=0),
        )(*pair)
    mixed = call(
        conv_kernel,
        jax.ShapeDtypeStruct((PARTS, 4, CH, 128), BF16),
        [
            pltpu.VMEM((AT_ONCE, 256, 256), F32),
            pltpu.VMEM((32 * PITCH, 128), F32),
        ],
    )(*[t for t, _ in tiles], *[w for _, w in tiles])
    back = exchange_far_first(mixed)
    return call(
        gate_kernel,
        jax.ShapeDtypeStruct((512, 256), BF16),
        [
            pltpu.VMEM((PARTS, 4, CH, 128), BF16),
            pltpu.VMEM((512, 256), BF16),
            pltpu.SemaphoreType.DMA((4,)),
        ],
        out_specs=pl.BlockSpec(memory_space=pl.ANY),
    )(*[y for pair in back for y in pair], direct, gate_branch)


def solution(mesh):
    in_specs = (P("seq", "ch"), P("seq", "ch"), P("seq", "ch"), P("seq", "ch"), P("ch"))
    return jax.shard_map(
        on_device, mesh=mesh, in_specs=in_specs, out_specs=P("seq", "ch"), check_vma=False
    )
```

```python
import jax
import jax.numpy as jnp
from jax import lax
from jax.experimental import pallas as pl
from jax.experimental.pallas import tpu as pltpu
from jax.sharding import PartitionSpec as P

F32 = jnp.float32
BF16 = jnp.bfloat16
PARTS = 8
CH = 32
AT_ONCE = 8
BEHIND = 4
SPREAD_AT_ONCE = 32
PITCH = 40
VMEM = 24 * 1024 * 1024


def slot_of(j):
    return lax.select(j >= 6, j, lax.rem(j + 2, 6))


def pack_kernel(p_ref, f_ref, o_s):
    me = lax.axis_index("seq")
    p = p_ref[...].astype(F32)
    p = p.reshape(4, 8, 16, 256)
    p = jnp.stack([p[3 - a] for a in range(4)], 1).reshape(512, 256)
    f = f_ref[...].astype(F32)
    for half in range(2):
        for q in range(4):
            for at, x in ((0, p), (4, f)):
                block = x[128 * q : 128 * q + 128, 128 * half : 128 * half + 128]
                block = block.T.astype(BF16).reshape(4, CH, 128)
                for t in range(4):
                    o_s[slot_of(lax.bitwise_xor(me, 4 * half + t)), at + q] = block[t]


def both(refs):
    return refs if len(refs) == 2 else (refs[0].at[0], refs[0].at[1])


def spread_kernel(*refs):
    pair, (t_ref, w_ref, g_s, v_s) = both(refs[:-4]), refs[-4:]
    odd = lax.rem(lax.axis_index("seq"), 2)
    lane = lax.broadcasted_iota(jnp.int32, (32, 128), 1)
    row = lax.broadcasted_iota(jnp.int32, (32, 128), 0)
    for j, at in ((0, odd), (1, 1 - odd)):
        at = pl.multiple_of(4 * CH * at, 4 * CH)
        g_s[pl.ds(at, 4 * CH)] = pair[j][4:8].astype(F32).reshape(4 * CH, 128)
    mine, other = pair[0][0:4].astype(F32), pair[1][0:4].astype(F32)
    firsts, seconds = jnp.where(odd == 1, mine, other), jnp.where(odd == 1, other, mine)
    for q in range(4):
        first, second = firsts[q], seconds[q]
        swapped = pltpu.roll(jnp.where(lane < 64, second, first), 64, 1)
        at = 2 * CH * q
        v_s[at : at + CH] = jnp.where(lane < 64, first, swapped)
        v_s[at + CH : at + 2 * CH] = jnp.where(lane < 64, swapped, second)
    stay_a = lane[:16] < 16 + 16 * (row[:16] % 8)
    stay_b = lane[:16] >= row[:16]

    def spread(c):
        prev = jnp.zeros((16, 128), F32)
        for g in range(8):
            taps = jnp.broadcast_to(g_s[pl.ds(CH * g + c, 1), :], (16, 128))
            rot = pltpu.roll(taps, 0, 1, stride=1, stride_axis=0)
            t_ref[c, 16 * g : 16 * g + 16] = jnp.where(stay_b, rot, prev).astype(BF16)
            prev = rot
        t_ref[c, 128:144] = jnp.where(stay_b, 0.0, prev).astype(BF16)
        for b in range(0, 8, 2):
            rots = []
            for j in range(2):
                vals = jnp.broadcast_to(v_s[pl.ds(CH * (b + j) + c, 1), :], (8, 128))
                rots.append(pltpu.roll(vals, 16, 1, stride=16, stride_axis=0))
            rot = jnp.concatenate(rots, 0)
            w_ref[c, 8 * b : 8 * b + 16] = jnp.where(stay_a, rot, 0.0).astype(BF16)
            w_ref[c, 64 + 8 * b : 80 + 8 * b] = jnp.where(stay_a, 0.0, rot).astype(BF16)

    def step(i, carry):
        for u in range(SPREAD_AT_ONCE):
            spread(i * SPREAD_AT_ONCE + u)
        return carry

    lax.fori_loop(0, CH // SPREAD_AT_ONCE, step, 0)


def conv_kernel(*refs):
    ts, ws, (y_ref, o_s, y_s) = refs[:4], refs[4:8], refs[8:]
    me = lax.axis_index("seq")
    z = lax.div(me, 2)
    for at in range(4):
        order = [at ^ chip for chip in range(4)]

        @pl.when(z == at)
        def _(order=order):
            convolve([ts[i] for i in order], [ws[i] for i in order], o_s, y_s)

    for s in range(PARTS):
        for q in range(4):
            at = PITCH * (4 * s + q)
            y_ref[slot_of(lax.bitwise_xor(me, s)), q] = y_s[at : at + CH].astype(BF16)


def convolve(ts, ws, o_s, y_s):
    lane = lax.broadcasted_iota(jnp.int32, (32, 128), 1)
    row = lax.broadcasted_iota(jnp.int32, (32, 128), 0)

    def multiply(c, u):
        right = [ts[0][c, 0:128]]
        for j in range(1, 4):
            first = ts[j][c, 0:16] + ts[j - 1][c, 128:144]
            right.append(jnp.concatenate([first, ts[j][c, 16:128]], 0))
        right = jnp.concatenate(
            [jnp.concatenate(right[0:2], 0), jnp.concatenate(right[2:4], 0)], 1
        )
        w = [ws[0][c, 0:64]] + [ws[j][c, 0:64] + ws[j - 1][c, 64:128] for j in range(1, 4)]
        zero = jnp.zeros((64, 128), BF16)
        left = jnp.concatenate(
            [jnp.concatenate([w[j], w[j - 1] if j else zero], 1) for j in range(4)], 0
        )
        o_s[u] = jnp.dot(left, right, preferred_element_type=F32)

    def collect(c, u):
        here = jnp.zeros((32, 128), F32)
        late = jnp.zeros((32, 128), F32)
        for b in range(8):
            r = []
            for j in range(4):
                part = o_s[u, 64 * j + 8 * b : 64 * j + 8 * b + 8, :128]
                if j >= 2:
                    at = 64 * (j - 2) + 8 * b
                    part = part + o_s[u, at : at + 8, 128:]
                r.append(part)
            r = jnp.concatenate(r, 0)
            if b:
                r = pltpu.roll(r, 16 * b, 1)
                over = lane < 16 * b
                late = late + jnp.where(over, r, 0.0)
                r = jnp.where(over, 0.0, r)
            here = here + r
        late = jnp.where(row == 0, 0.0, pltpu.roll(late, 1, 0))
        y_s[pl.ds(c, 32, stride=PITCH), :] = here + late

    for c in range(CH):
        multiply(c, c % AT_ONCE)
        if c >= BEHIND:
            collect(c - BEHIND, (c - BEHIND) % AT_ONCE)
    for c in range(CH - BEHIND, CH):
        collect(c, c % AT_ONCE)


def gate_kernel(*refs):
    y_refs, (d_ref, g_ref, o_ref, y_s, o_s, sem) = refs[:-6], refs[-6:]
    me = lax.axis_index("seq")
    pairs = [both(y_refs[i : i + n]) for i, n in ((0, 1), (1, 1), (2, 2), (4, 1))]
    for s in range(PARTS):
        y_s[lax.bitwise_xor(me, s)] = pairs[s // 2][s % 2][...]
    copies = []
    for q in range(4):
        pos = slice(128 * q, 128 * q + 128)
        for half in range(2):
            ch = slice(128 * half, 128 * half + 128)
            y = y_s[4 * half : 4 * half + 4, q].reshape(128, 128).astype(F32).T
            out = g_ref[pos, ch].astype(F32) * (y + d_ref[pos, ch])
            o_s[pos, ch] = out.astype(BF16)
        copies.append(pltpu.make_async_copy(o_s.at[pos], o_ref.at[pos], sem.at[q]))
        copies[-1].start()
    for copy in copies:
        copy.wait()


def call(kernel, out, scratch=(), limit=VMEM, **more):
    return pl.pallas_call(
        kernel,
        out_shape=out,
        scratch_shapes=scratch,
        compiler_params=pltpu.CompilerParams(vmem_limit_bytes=limit),
        **more,
    )


def swap(x, j):
    return lax.ppermute(x, "seq", [(i, i ^ j) for i in range(PARTS)])


def exchange(x):
    x = x.reshape(4, 2, *x.shape[1:])
    far = swap(x[0], 4)
    other = swap(x[1:, 1], 1)
    near = jnp.stack([x[1:, 0], other], 1)
    return [
        (near[0],),
        (swap(near[1], 2),),
        (far[0], swap(far[1], 1)),
        (swap(near[2], 6),),
    ]


def on_device(key_branch, value_branch, gate_branch, conv_filter, skip_gain):
    product = key_branch.astype(F32) * value_branch.astype(F32)
    product = lax.reduce_precision(product, 8, 7)
    direct = skip_gain[None, :] * product
    product = product.astype(BF16)
    sent = call(pack_kernel, jax.ShapeDtypeStruct((PARTS, 8, CH, 128), BF16))(
        product, conv_filter
    )
    pairs = exchange(sent)
    tiles = [None] * 4
    for last, i in ((None, 0), (0, 3), (3, 1), (1, 2)):
        pair = pairs[i]
        if last is not None:
            pair, tiles[last] = lax.optimization_barrier((pair, tiles[last]))
        tiles[i] = call(
            spread_kernel,
            [
                jax.ShapeDtypeStruct((CH, 144, 128), BF16),
                jax.ShapeDtypeStruct((CH, 128, 128), BF16),
            ],
            [pltpu.VMEM((8 * CH, 128), F32)] * 2,
            cost_estimate=pl.CostEstimate(flops=10**8, bytes_accessed=3 * 10**6, transcendentals=0),
        )(*pair)
    mixed = call(
        conv_kernel,
        jax.ShapeDtypeStruct((PARTS, 4, CH, 128), BF16),
        [
            pltpu.VMEM((AT_ONCE, 256, 256), F32),
            pltpu.VMEM((32 * PITCH, 128), F32),
        ],
    )(*[t for t, _ in tiles], *[w for _, w in tiles])
    back = exchange(mixed)
    return call(
        gate_kernel,
        jax.ShapeDtypeStruct((512, 256), BF16),
        [
            pltpu.VMEM((PARTS, 4, CH, 128), BF16),
            pltpu.VMEM((512, 256), BF16),
            pltpu.SemaphoreType.DMA((4,)),
        ],
        out_specs=pl.BlockSpec(memory_space=pl.ANY),
    )(*[y for pair in back for y in pair], direct, gate_branch)


def solution(mesh):
    in_specs = (P("seq", "ch"), P("seq", "ch"), P("seq", "ch"), P("seq", "ch"), P("ch"))
    return jax.shard_map(
        on_device, mesh=mesh, in_specs=in_specs, out_specs=P("seq", "ch"), check_vma=False
    )
```

```python
import jax
import jax.numpy as jnp
from jax import lax
from jax.experimental import pallas as pl
from jax.experimental.pallas import tpu as pltpu
from jax.sharding import PartitionSpec as P

F32 = jnp.float32
BF16 = jnp.bfloat16
PARTS = 8
CH = 32
AT_ONCE = 8
BEHIND = 4
SPREAD_AT_ONCE = 32
PITCH = 40
VMEM = 24 * 1024 * 1024


def slot_of(j):
    return lax.select(j >= 6, j, lax.rem(j + 2, 6))


def pack_kernel(p_ref, f_ref, o_s):
    me = lax.axis_index("seq")
    p = p_ref[...].astype(F32)
    p = p.reshape(4, 8, 16, 256)
    p = jnp.stack([p[3 - a] for a in range(4)], 1).reshape(512, 256)
    f = f_ref[...].astype(F32)
    for half in range(2):
        for q in range(4):
            for at, x in ((0, p), (4, f)):
                block = x[128 * q : 128 * q + 128, 128 * half : 128 * half + 128]
                block = block.T.astype(BF16).reshape(4, CH, 128)
                for t in range(4):
                    o_s[slot_of(lax.bitwise_xor(me, 4 * half + t)), at + q] = block[t]


def both(refs):
    return refs if len(refs) == 2 else (refs[0].at[0], refs[0].at[1])


def spread_kernel(*refs):
    pair, (t_ref, w_ref, g_s, v_s) = both(refs[:-4]), refs[-4:]
    odd = lax.rem(lax.axis_index("seq"), 2)
    lane = lax.broadcasted_iota(jnp.int32, (32, 128), 1)
    row = lax.broadcasted_iota(jnp.int32, (32, 128), 0)
    for j, at in ((0, odd), (1, 1 - odd)):
        at = pl.multiple_of(4 * CH * at, 4 * CH)
        g_s[pl.ds(at, 4 * CH)] = pair[j][4:8].astype(F32).reshape(4 * CH, 128)
    mine, other = pair[0][0:4].astype(F32), pair[1][0:4].astype(F32)
    firsts, seconds = jnp.where(odd == 1, mine, other), jnp.where(odd == 1, other, mine)
    for q in range(4):
        first, second = firsts[q], seconds[q]
        swapped = pltpu.roll(jnp.where(lane < 64, second, first), 64, 1)
        at = 2 * CH * q
        v_s[at : at + CH] = jnp.where(lane < 64, first, swapped)
        v_s[at + CH : at + 2 * CH] = jnp.where(lane < 64, swapped, second)
    stay_a = lane[:16] < 16 + 16 * (row[:16] % 8)
    stay_b = lane[:16] >= row[:16]

    def spread(c):
        prev = jnp.zeros((16, 128), F32)
        for g in range(8):
            taps = jnp.broadcast_to(g_s[pl.ds(CH * g + c, 1), :], (16, 128))
            rot = pltpu.roll(taps, 0, 1, stride=1, stride_axis=0)
            t_ref[c, 16 * g : 16 * g + 16] = jnp.where(stay_b, rot, prev).astype(BF16)
            prev = rot
        t_ref[c, 128:144] = jnp.where(stay_b, 0.0, prev).astype(BF16)
        for b in range(0, 8, 2):
            rots = []
            for j in range(2):
                vals = jnp.broadcast_to(v_s[pl.ds(CH * (b + j) + c, 1), :], (8, 128))
                rots.append(pltpu.roll(vals, 16, 1, stride=16, stride_axis=0))
            rot = jnp.concatenate(rots, 0)
            w_ref[c, 8 * b : 8 * b + 16] = jnp.where(stay_a, rot, 0.0).astype(BF16)
            w_ref[c, 64 + 8 * b : 80 + 8 * b] = jnp.where(stay_a, 0.0, rot).astype(BF16)

    def step(i, carry):
        for u in range(SPREAD_AT_ONCE):
            spread(i * SPREAD_AT_ONCE + u)
        return carry

    lax.fori_loop(0, CH // SPREAD_AT_ONCE, step, 0)


def conv_kernel(*refs):
    ts, ws, (y_ref, o_s, y_s) = refs[:4], refs[4:8], refs[8:]
    me = lax.axis_index("seq")
    z = lax.div(me, 2)
    for at in range(4):
        order = [at ^ chip for chip in range(4)]

        @pl.when(z == at)
        def _(order=order):
            convolve([ts[i] for i in order], [ws[i] for i in order], o_s, y_s)

    for s in range(PARTS):
        for q in range(4):
            at = PITCH * (4 * s + q)
            y_ref[slot_of(lax.bitwise_xor(me, s)), q] = y_s[at : at + CH].astype(BF16)


def convolve(ts, ws, o_s, y_s):
    lane = lax.broadcasted_iota(jnp.int32, (32, 128), 1)
    row = lax.broadcasted_iota(jnp.int32, (32, 128), 0)

    def multiply(c, u):
        right = [ts[0][c, 0:128]]
        for j in range(1, 4):
            first = ts[j][c, 0:16] + ts[j - 1][c, 128:144]
            right.append(jnp.concatenate([first, ts[j][c, 16:128]], 0))
        right = jnp.concatenate(
            [jnp.concatenate(right[0:2], 0), jnp.concatenate(right[2:4], 0)], 1
        )
        w = [ws[0][c, 0:64]] + [ws[j][c, 0:64] + ws[j - 1][c, 64:128] for j in range(1, 4)]
        zero = jnp.zeros((64, 128), BF16)
        left = jnp.concatenate(
            [jnp.concatenate([w[j], w[j - 1] if j else zero], 1) for j in range(4)], 0
        )
        o_s[u] = jnp.dot(left, right, preferred_element_type=F32)

    def collect(c, u):
        here = jnp.zeros((32, 128), F32)
        late = jnp.zeros((32, 128), F32)
        for b in range(8):
            r = []
            for j in range(4):
                part = o_s[u, 64 * j + 8 * b : 64 * j + 8 * b + 8, :128]
                if j >= 2:
                    at = 64 * (j - 2) + 8 * b
                    part = part + o_s[u, at : at + 8, 128:]
                r.append(part)
            r = jnp.concatenate(r, 0)
            if b:
                r = pltpu.roll(r, 16 * b, 1)
                over = lane < 16 * b
                late = late + jnp.where(over, r, 0.0)
                r = jnp.where(over, 0.0, r)
            here = here + r
        late = jnp.where(row == 0, 0.0, pltpu.roll(late, 1, 0))
        y_s[pl.ds(c, 32, stride=PITCH), :] = here + late

    for c in range(CH):
        multiply(c, c % AT_ONCE)
        if c >= BEHIND:
            collect(c - BEHIND, (c - BEHIND) % AT_ONCE)
    for c in range(CH - BEHIND, CH):
        collect(c, c % AT_ONCE)


def gate_kernel(*refs):
    y_refs, (d_ref, g_ref, o_ref, y_s, o_s, sem) = refs[:-6], refs[-6:]
    me = lax.axis_index("seq")
    pairs = [both(y_refs[i : i + n]) for i, n in ((0, 1), (1, 1), (2, 2), (4, 1))]
    for s in range(PARTS):
        y_s[lax.bitwise_xor(me, s)] = pairs[s // 2][s % 2][...]
    copies = []
    for q in range(4):
        pos = slice(128 * q, 128 * q + 128)
        for half in range(2):
            ch = slice(128 * half, 128 * half + 128)
            y = y_s[4 * half : 4 * half + 4, q].reshape(128, 128).astype(F32).T
            out = g_ref[pos, ch].astype(F32) * (y + d_ref[pos, ch])
            o_s[pos, ch] = out.astype(BF16)
        copies.append(pltpu.make_async_copy(o_s.at[pos], o_ref.at[pos], sem.at[q]))
        copies[-1].start()
    for copy in copies:
        copy.wait()


def call(kernel, out, scratch=(), limit=VMEM, **more):
    return pl.pallas_call(
        kernel,
        out_shape=out,
        scratch_shapes=scratch,
        compiler_params=pltpu.CompilerParams(vmem_limit_bytes=limit),
        **more,
    )


def swap(x, j):
    return lax.ppermute(x, "seq", [(i, i ^ j) for i in range(PARTS)])


def exchange(x):
    x = x.reshape(4, 2, *x.shape[1:])
    far = swap(x[0], 4)
    other = swap(x[1:, 1], 1)
    near = jnp.stack([x[1:, 0], other], 1)
    return [
        (near[0],),
        (swap(near[1], 2),),
        (far[0], swap(far[1], 1)),
        (swap(near[2], 6),),
    ]


def on_device(key_branch, value_branch, gate_branch, conv_filter, skip_gain):
    product = key_branch.astype(F32) * value_branch.astype(F32)
    product = lax.reduce_precision(product, 8, 7)
    direct = skip_gain[None, :] * product
    product = product.astype(BF16)
    sent = call(pack_kernel, jax.ShapeDtypeStruct((PARTS, 8, CH, 128), BF16))(
        product, conv_filter
    )
    pairs = exchange(sent)
    tiles = [None] * 4
    for last, i in ((None, 0), (0, 2), (2, 3), (3, 1)):
        pair = pairs[i]
        if last is not None:
            pair, tiles[last] = lax.optimization_barrier((pair, tiles[last]))
        tiles[i] = call(
            spread_kernel,
            [
                jax.ShapeDtypeStruct((CH, 144, 128), BF16),
                jax.ShapeDtypeStruct((CH, 128, 128), BF16),
            ],
            [pltpu.VMEM((8 * CH, 128), F32)] * 2,
            cost_estimate=pl.CostEstimate(flops=10**8, bytes_accessed=3 * 10**6, transcendentals=0),
        )(*pair)
    mixed = call(
        conv_kernel,
        jax.ShapeDtypeStruct((PARTS, 4, CH, 128), BF16),
        [
            pltpu.VMEM((AT_ONCE, 256, 256), F32),
            pltpu.VMEM((32 * PITCH, 128), F32),
        ],
    )(*[t for t, _ in tiles], *[w for _, w in tiles])
    back = exchange(mixed)
    return call(
        gate_kernel,
        jax.ShapeDtypeStruct((512, 256), BF16),
        [
            pltpu.VMEM((PARTS, 4, CH, 128), BF16),
            pltpu.VMEM((512, 256), BF16),
            pltpu.SemaphoreType.DMA((4,)),
        ],
        out_specs=pl.BlockSpec(memory_space=pl.ANY),
    )(*[y for pair in back for y in pair], direct, gate_branch)


def solution(mesh):
    in_specs = (P("seq", "ch"), P("seq", "ch"), P("seq", "ch"), P("seq", "ch"), P("ch"))
    return jax.shard_map(
        on_device, mesh=mesh, in_specs=in_specs, out_specs=P("seq", "ch"), check_vma=False
    )
```

```python
import jax
import jax.numpy as jnp
from jax import lax
from jax.experimental import pallas as pl
from jax.experimental.pallas import tpu as pltpu
from jax.sharding import PartitionSpec as P

F32 = jnp.float32
BF16 = jnp.bfloat16
PARTS = 8
CH = 32
AT_ONCE = 8
BEHIND = 4
SPREAD_AT_ONCE = 32
PITCH = 40
VMEM = 24 * 1024 * 1024


def slot_of(j):
    return lax.select(j >= 6, j, lax.rem(j + 2, 6))


def pack_kernel(p_ref, f_ref, o_s):
    me = lax.axis_index("seq")
    p = p_ref[...].astype(F32)
    p = p.reshape(4, 8, 16, 256)
    p = jnp.stack([p[3 - a] for a in range(4)], 1).reshape(512, 256)
    f = f_ref[...].astype(F32)
    for half in range(2):
        for q in range(4):
            for at, x in ((0, p), (4, f)):
                block = x[128 * q : 128 * q + 128, 128 * half : 128 * half + 128]
                block = block.T.astype(BF16).reshape(4, CH, 128)
                for t in range(4):
                    o_s[slot_of(lax.bitwise_xor(me, 4 * half + t)), at + q] = block[t]


def both(refs):
    return refs if len(refs) == 2 else (refs[0].at[0], refs[0].at[1])


def spread_kernel(*refs):
    pair, (t_ref, w_ref, g_s, v_s) = both(refs[:-4]), refs[-4:]
    odd = lax.rem(lax.axis_index("seq"), 2)
    lane = lax.broadcasted_iota(jnp.int32, (32, 128), 1)
    row = lax.broadcasted_iota(jnp.int32, (32, 128), 0)
    for j, at in ((0, odd), (1, 1 - odd)):
        at = pl.multiple_of(4 * CH * at, 4 * CH)
        g_s[pl.ds(at, 4 * CH)] = pair[j][4:8].astype(F32).reshape(4 * CH, 128)
    mine, other = pair[0][0:4].astype(F32), pair[1][0:4].astype(F32)
    firsts, seconds = jnp.where(odd == 1, mine, other), jnp.where(odd == 1, other, mine)
    for q in range(4):
        first, second = firsts[q], seconds[q]
        swapped = pltpu.roll(jnp.where(lane < 64, second, first), 64, 1)
        at = 2 * CH * q
        v_s[at : at + CH] = jnp.where(lane < 64, first, swapped)
        v_s[at + CH : at + 2 * CH] = jnp.where(lane < 64, swapped, second)
    stay_a = lane[:16] < 16 + 16 * (row[:16] % 8)
    stay_b = lane[:16] >= row[:16]

    def spread(c):
        prev = jnp.zeros((16, 128), F32)
        for g in range(8):
            taps = jnp.broadcast_to(g_s[pl.ds(CH * g + c, 1), :], (16, 128))
            rot = pltpu.roll(taps, 0, 1, stride=1, stride_axis=0)
            t_ref[c, 16 * g : 16 * g + 16] = jnp.where(stay_b, rot, prev).astype(BF16)
            prev = rot
        t_ref[c, 128:144] = jnp.where(stay_b, 0.0, prev).astype(BF16)
        for b in range(0, 8, 2):
            rots = []
            for j in range(2):
                vals = jnp.broadcast_to(v_s[pl.ds(CH * (b + j) + c, 1), :], (8, 128))
                rots.append(pltpu.roll(vals, 16, 1, stride=16, stride_axis=0))
            rot = jnp.concatenate(rots, 0)
            w_ref[c, 8 * b : 8 * b + 16] = jnp.where(stay_a, rot, 0.0).astype(BF16)
            w_ref[c, 64 + 8 * b : 80 + 8 * b] = jnp.where(stay_a, 0.0, rot).astype(BF16)

    def step(i, carry):
        for u in range(SPREAD_AT_ONCE):
            spread(i * SPREAD_AT_ONCE + u)
        return carry

    lax.fori_loop(0, CH // SPREAD_AT_ONCE, step, 0)


def conv_kernel(*refs):
    ts, ws, (y_ref, o_s, y_s) = refs[:4], refs[4:8], refs[8:]
    me = lax.axis_index("seq")
    z = lax.div(me, 2)
    for at in range(4):
        order = [at ^ chip for chip in range(4)]

        @pl.when(z == at)
        def _(order=order):
            convolve([ts[i] for i in order], [ws[i] for i in order], o_s, y_s)

    for s in range(PARTS):
        for q in range(4):
            at = PITCH * (4 * s + q)
            y_ref[slot_of(lax.bitwise_xor(me, s)), q] = y_s[at : at + CH].astype(BF16)


def convolve(ts, ws, o_s, y_s):
    lane = lax.broadcasted_iota(jnp.int32, (32, 128), 1)
    row = lax.broadcasted_iota(jnp.int32, (32, 128), 0)

    def multiply(c, u):
        right = [ts[0][c, 0:128]]
        for j in range(1, 4):
            first = ts[j][c, 0:16] + ts[j - 1][c, 128:144]
            right.append(jnp.concatenate([first, ts[j][c, 16:128]], 0))
        right = jnp.concatenate(
            [jnp.concatenate(right[0:2], 0), jnp.concatenate(right[2:4], 0)], 1
        )
        w = [ws[0][c, 0:64]] + [ws[j][c, 0:64] + ws[j - 1][c, 64:128] for j in range(1, 4)]
        zero = jnp.zeros((64, 128), BF16)
        left = jnp.concatenate(
            [jnp.concatenate([w[j], w[j - 1] if j else zero], 1) for j in range(4)], 0
        )
        o_s[u] = jnp.dot(left, right, preferred_element_type=F32)

    def collect(c, u):
        here = jnp.zeros((32, 128), F32)
        late = jnp.zeros((32, 128), F32)
        for b in range(8):
            r = []
            for j in range(4):
                part = o_s[u, 64 * j + 8 * b : 64 * j + 8 * b + 8, :128]
                if j >= 2:
                    at = 64 * (j - 2) + 8 * b
                    part = part + o_s[u, at : at + 8, 128:]
                r.append(part)
            r = jnp.concatenate(r, 0)
            if b:
                r = pltpu.roll(r, 16 * b, 1)
                over = lane < 16 * b
                late = late + jnp.where(over, r, 0.0)
                r = jnp.where(over, 0.0, r)
            here = here + r
        late = jnp.where(row == 0, 0.0, pltpu.roll(late, 1, 0))
        y_s[pl.ds(c, 32, stride=PITCH), :] = here + late

    for c in range(CH):
        multiply(c, c % AT_ONCE)
        if c >= BEHIND:
            collect(c - BEHIND, (c - BEHIND) % AT_ONCE)
    for c in range(CH - BEHIND, CH):
        collect(c, c % AT_ONCE)


def gate_kernel(*refs):
    y_refs, (d_ref, g_ref, o_ref, y_s, o_s, sem) = refs[:-6], refs[-6:]
    me = lax.axis_index("seq")
    pairs = [both(y_refs[i : i + n]) for i, n in ((0, 1), (1, 1), (2, 2), (4, 1))]
    for s in range(PARTS):
        y_s[lax.bitwise_xor(me, s)] = pairs[s // 2][s % 2][...]
    copies = []
    for q in range(4):
        pos = slice(128 * q, 128 * q + 128)
        for half in range(2):
            ch = slice(128 * half, 128 * half + 128)
            y = y_s[4 * half : 4 * half + 4, q].reshape(128, 128).astype(F32).T
            out = g_ref[pos, ch].astype(F32) * (y + d_ref[pos, ch])
            o_s[pos, ch] = out.astype(BF16)
        copies.append(pltpu.make_async_copy(o_s.at[pos], o_ref.at[pos], sem.at[q]))
        copies[-1].start()
    for copy in copies:
        copy.wait()


def call(kernel, out, scratch=(), limit=VMEM, **more):
    return pl.pallas_call(
        kernel,
        out_shape=out,
        scratch_shapes=scratch,
        compiler_params=pltpu.CompilerParams(vmem_limit_bytes=limit),
        **more,
    )


def swap(x, j):
    return lax.ppermute(x, "seq", [(i, i ^ j) for i in range(PARTS)])


def exchange(x):
    x = x.reshape(4, 2, *x.shape[1:])
    far = swap(x[0], 4)
    other = swap(x[1:, 1], 1)
    near = jnp.stack([x[1:, 0], other], 1)
    return [
        (near[0],),
        (swap(near[1], 2),),
        (far[0], swap(far[1], 1)),
        (swap(near[2], 6),),
    ]


def on_device(key_branch, value_branch, gate_branch, conv_filter, skip_gain):
    product = key_branch.astype(F32) * value_branch.astype(F32)
    product = lax.reduce_precision(product, 8, 7)
    direct = skip_gain[None, :] * product
    product = product.astype(BF16)
    sent = call(pack_kernel, jax.ShapeDtypeStruct((PARTS, 8, CH, 128), BF16))(
        product, conv_filter
    )
    pairs = exchange(sent)
    tiles = [None] * 4
    for last, i in ((None, 0), (0, 2), (2, 1), (1, 3)):
        pair = pairs[i]
        if last is not None:
            pair, tiles[last] = lax.optimization_barrier((pair, tiles[last]))
        tiles[i] = call(
            spread_kernel,
            [
                jax.ShapeDtypeStruct((CH, 144, 128), BF16),
                jax.ShapeDtypeStruct((CH, 128, 128), BF16),
            ],
            [pltpu.VMEM((8 * CH, 128), F32)] * 2,
            cost_estimate=pl.CostEstimate(flops=10**8, bytes_accessed=3 * 10**6, transcendentals=0),
        )(*pair)
    mixed = call(
        conv_kernel,
        jax.ShapeDtypeStruct((PARTS, 4, CH, 128), BF16),
        [
            pltpu.VMEM((AT_ONCE, 256, 256), F32),
            pltpu.VMEM((32 * PITCH, 128), F32),
        ],
    )(*[t for t, _ in tiles], *[w for _, w in tiles])
    back = exchange(mixed)
    return call(
        gate_kernel,
        jax.ShapeDtypeStruct((512, 256), BF16),
        [
            pltpu.VMEM((PARTS, 4, CH, 128), BF16),
            pltpu.VMEM((512, 256), BF16),
            pltpu.SemaphoreType.DMA((4,)),
        ],
        out_specs=pl.BlockSpec(memory_space=pl.ANY),
    )(*[y for pair in back for y in pair], direct, gate_branch)


def solution(mesh):
    in_specs = (P("seq", "ch"), P("seq", "ch"), P("seq", "ch"), P("seq", "ch"), P("ch"))
    return jax.shard_map(
        on_device, mesh=mesh, in_specs=in_specs, out_specs=P("seq", "ch"), check_vma=False
    )
```
